256 devices in a mesh: row: 4 (over x), col: 32 (over y, z), rep: 2 (over core).
Axes of the slice: x: 4, y: 4, z: 8, core: 2. Of those that a mesh axis runs over, the one named last changes fastest.
Arguments:
- amplitudes: bfloat16 [16384, 16384], P(('row', 'col'), 'rep'), may hold values from -6 to 6
- cycle_integrals: bfloat16 [16384, 1024], P('rep', ('row', 'col')), may hold values from -0.046875 to 0.046875
- amp_map: int32 [128, 128], P(('row', 'col'), 'rep'), may hold values 0 or 1
- cycle_map: int32 [128, 128], replicated, may hold values 0 or 1
Outputs:
- dressed: bfloat16 [16384, 1024], P(('row', 'col'), 'rep')
- quadratic: bfloat16 [16384, 16384], P(('row', 'col'), 'rep')
The draws below stay inside these ranges and needn't reach their ends.
All inputs are finite; a program needn't handle non-finite values. No bound on the sum of `amp_map` on one device may be relied on, other than what follows from the above.
Results may differ from the reference program's by a relative error of at most 0.0049.
Values may be sent and summed in bfloat16 or wider, within the bound.
No kernel may reach another device: no remote copies, remote signals or barrier semaphores. Data moves between devices by JAX's collectives and lax.ppermute only.
A program may use at most 128 MiB of HBM per device.

```python
import jax
import jax.numpy as jnp
from jax import lax

TB = 128
P_DEV = 128
WD = 8
PAIRS = 16384
RW = 16384
QW = 1024
N_ROW = 4
N_COL = 32


def with_ends(result, key, least, top_value):
    shape = result.shape
    place = [jax.random.randint(jax.random.fold_in(key, axis), (), 0, shape[axis]) for axis in range(len(shape))]
    result = result.at[tuple(place)].set(least)
    longest = shape.index(max(shape))
    place[longest] = (place[longest] + 1) % shape[longest]
    return result.at[tuple(place)].set(top_value)


def block_scale(rng, shape, split, least, largest):
    def one(axis_at, blocks):
        heights = jax.random.uniform(jax.random.fold_in(jax.random.fold_in(rng, 6), axis_at), (blocks,), jnp.float32, least / len(split), largest / len(split))
        return jnp.repeat(jnp.exp(heights), shape[axis_at] // blocks).reshape((-1,) + (1,) * (len(shape) - axis_at - 1))

    gain = one(*split[0])
    for cut in split[1:]:
        gain = gain * one(*cut)
    return gain


def scatter_about(stream_key, extent, deviation, reach, shards=(), kind=jnp.bfloat16):
    values = deviation * jax.random.normal(stream_key, extent, jnp.float32)
    if shards:
        values = values * block_scale(stream_key, extent, shards, -0.22, 0.18)
    return jnp.clip(values, -reach, reach).astype(kind)


def setup_inputs(seed: int = 0) -> dict:
    key_list = jax.random.split(jax.random.key(seed), 5)
    return {
        "amplitudes": scatter_about(key_list[0], (PAIRS, RW), 1.0, 6.0, ((0, 128), (1, 2))),
        "cycle_integrals": scatter_about(key_list[1], (RW, QW), RW ** -0.5, 0.046875, ((0, 2), (1, 128))),
        "amp_map": with_ends((jax.random.randint(key_list[2], (PAIRS // TB, RW // TB), 0, 4) < 3).astype(jnp.int32), jax.random.fold_in(key_list[2], 1), 0, 1),
        "cycle_map": with_ends((jax.random.randint(key_list[3], (RW // TB, N_ROW * N_COL), 0, 4) < 3).astype(jnp.int32), jax.random.fold_in(key_list[3], 1), 0, 1),
    }


def expand(tile_map, rows, cols):
    return jnp.repeat(jnp.repeat(tile_map, rows, 0), cols, 1).astype(jnp.bfloat16)


def reference(amplitudes, cycle_integrals, amp_map, cycle_map):
    groups = N_ROW * N_COL
    cycle_masked = cycle_integrals * expand(cycle_map, TB, WD)
    amp_group = amplitudes.reshape(groups, P_DEV, RW)
    map_rows = jnp.repeat(amp_map, TB, 0).reshape(groups, P_DEV, RW // TB)
    window_mask = jnp.repeat(map_rows[:, :WD], TB, 2).astype(jnp.bfloat16)
    window = (amp_group[:, :WD] * window_mask).reshape(QW, RW)
    block_rows = P_DEV * N_ROW
    amp_blocks = amplitudes.reshape(N_COL, block_rows, RW)
    map_blocks = amp_map.reshape(N_COL, block_rows // TB, RW // TB)

    def one_block(pair):
        block, block_map = pair
        masked_amp = block * expand(block_map, TB, TB)
        dressed = jnp.dot(masked_amp, cycle_masked, preferred_element_type=jnp.float32).astype(jnp.bfloat16)
        quadratic = jnp.dot(dressed, window, preferred_element_type=jnp.float32).astype(jnp.bfloat16)
        return dressed, quadratic

    dressed_all, quad_all = lax.map(one_block, (amp_blocks, map_blocks))
    return dressed_all.reshape(PAIRS, QW), quad_all.reshape(PAIRS, RW)
```

```python
import jax
import jax.numpy as jnp
from jax import lax
from jax.sharding import PartitionSpec as P

TB = 128
WD = 8
NX, NY, NZ = 4, 4, 8
AX = ("row", "col", "rep")
F32, BF = jnp.float32, jnp.bfloat16


def ident(x, y, z, c):
    return ((x % NX) * NY * NZ + (y % NY) * NZ + z % NZ) * 2 + c


def every():
    return [(x, y, z, c) for x in range(NX) for y in range(NY) for z in range(NZ) for c in (0, 1)]


def shift_z(value, step):
    return lax.ppermute(value, AX, [(ident(x, y, z, c), ident(x, y, z + step, c)) for x, y, z, c in every()])


def shift_plane(value, step, swapped):
    pairs = []
    for x, y, z, c in every():
        if (c == 0) != swapped:
            pairs.append((ident(x, y, z, c), ident(x + step, y, z, c)))
        else:
            pairs.append((ident(x, y, z, c), ident(x, y + step, z, c)))
    return lax.ppermute(value, AX, pairs)


def shift_g(value, step):
    return shift_plane(value, step, False)


def shift_p(value, step):
    return shift_plane(value, step, True)


def swap_core(value):
    return lax.ppermute(value, AX, [(ident(x, y, z, c), ident(x, y, z, 1 - c)) for x, y, z, c in every()])


def unroll_ring(pieces, place):
    count, rows = len(pieces), pieces[0].shape[0]
    twice = jnp.concatenate(pieces + pieces, 0)
    return lax.dynamic_slice_in_dim(twice, ((count - place) % count) * rows, count * rows, 0)


def body(amplitudes, cycle_integrals, amp_map, cycle_map):
    row, col, core = (lax.axis_index(a) for a in AX)
    x, y, z = row, col // NZ, col % NZ
    g = jnp.where(core == 0, x, y)
    p = jnp.where(core == 0, y, x)
    half = amplitudes.shape[1]
    part = half // 4

    amp_mask = jnp.repeat(amp_map, TB, 1).astype(BF)

    def columns(value, index):
        return lax.dynamic_slice_in_dim(value, (index % 4) * part, part, 1)

    sends = [columns(amplitudes, g + d) * columns(amp_mask, g + d) for d in range(4)]
    blocks = [sends[0]] + [shift_g(sends[d], d) for d in (1, 2, 3)]

    tiles = half // TB
    own_column = lax.dynamic_slice(cycle_map, (core * tiles, row * NY * NZ + col), (tiles, 1))
    cyc = cycle_integrals.T * jnp.repeat(own_column.reshape(1, tiles), TB, 1).astype(BF)
    cyc = cyc.reshape(WD, 4, part).transpose(1, 0, 2)
    send = jnp.where(core == 0, cyc[:, None], cyc[None]).reshape(16 * WD, part)
    plane = [[i * NY * NZ + j * NZ + k for i in range(NX) for j in range(NY)] for k in range(NZ)]
    cyc = lax.all_to_all(send, ("row", "col"), 0, 0, tiled=True, axis_index_groups=plane)
    rings = [[j * NZ + k for k in range(NZ)] for j in range(NY)]
    cyc = lax.all_gather(cyc, "col", axis=0, tiled=True, axis_index_groups=rings)

    win = amplitudes[:WD] * amp_mask
    f, b = shift_z(win, 1), shift_z(win, -1)
    f2, b2 = shift_z(f, 1), shift_z(b, -1)
    f3, b3 = shift_z(f2, 1), shift_z(b2, -1)
    b4 = shift_z(b3, -1)
    win = unroll_ring([win, b, b2, b3, b4, f3, f2, f], z)
    pieces = [columns(win, g)] + [shift_g(columns(win, g - d), -d) for d in (1, 2, 3)]
    win = unroll_ring(pieces, g)
    f, b = shift_p(win, 1), shift_p(win, -1)
    rows = win.shape[0] // 2
    far = jnp.concatenate([shift_p(b[:rows], -1), shift_p(f[rows:], 1)], 0)
    win = unroll_ring([win, b, far, f], p)

    def times(a, b):
        return lax.dot_general(a, b, (((1,), (1,)), ((), ())), preferred_element_type=F32)

    total = times(blocks[0], cyc)
    for d in (2, 1, 3):
        total = total + shift_g(times(blocks[d], cyc).astype(BF), -d).astype(F32)
    full = (total + swap_core(total)).astype(BF)
    width = full.shape[1]
    here = lax.broadcasted_iota(jnp.int32, (width, 1), 0)
    hz, hx, hy, hw = here // 128, here // 32 % 4, here // 8 % 4, here % 8
    there = lax.broadcasted_iota(jnp.int32, (1, width // 2), 1) + core * (width // 2)
    place = hx * 256 + hy * 64 + hz * 8 + hw
    dressed = jnp.dot(full, (place == there).astype(BF), preferred_element_type=F32).astype(BF)
    hg, hp = jnp.where(core == 0, hx, hy), jnp.where(core == 0, hy, hx)
    place = hp * 256 + hg * 64 + hz * 8 + hw
    there = lax.broadcasted_iota(jnp.int32, (1, width), 1)
    inner = jnp.dot(full, (place == there).astype(BF), preferred_element_type=F32).astype(BF)

    inners = [inner] + [shift_g(inner, d) for d in (1, 2, 3)]
    outs = [None] * 4
    for d in (2, 1, 3, 0):
        value = jnp.dot(inners[d], win, preferred_element_type=F32).astype(BF)
        outs[d] = shift_g(value, -d) if d else value
    quadratic = jnp.zeros((inner.shape[0], half), BF)
    for d in range(4):
        quadratic = lax.dynamic_update_slice_in_dim(quadratic, outs[d], ((g + d) % 4) * part, 1)
    return (dressed, quadratic)


def solution(mesh):
    placed = (P(("row", "col"), "rep"), P("rep", ("row", "col")), P(("row", "col"), "rep"), P())
    return jax.shard_map(
        body,
        mesh=mesh,
        in_specs=placed,
        out_specs=(P(("row", "col"), "rep"), P(("row", "col"), "rep")),
        check_vma=False,
    )
```

```python
import functools

import jax
import jax.numpy as jnp
from jax import lax
from jax.experimental import pallas as pl
from jax.experimental.pallas import tpu as pltpu
from jax.sharding import PartitionSpec as P

TB = 128
WD = 8
NX, NY, NZ = 4, 4, 8
AX = ("row", "col", "rep")
F32, BF = jnp.float32, jnp.bfloat16
ROWS = 128
HALF = 8192
PART = HALF // 4
QW = 1024
VMEM = pl.BlockSpec(memory_space=pltpu.VMEM)
PARAMS = pltpu.CompilerParams(vmem_limit_bytes=40 * 2**20)


def ident(x, y, z, c):
    return ((x % NX) * NY * NZ + (y % NY) * NZ + z % NZ) * 2 + c


def every():
    return [(x, y, z, c) for x in range(NX) for y in range(NY) for z in range(NZ) for c in (0, 1)]


def shift_z(value, step):
    return lax.ppermute(value, AX, [(ident(x, y, z, c), ident(x, y, z + step, c)) for x, y, z, c in every()])


def shift_plane(value, step, swapped):
    pairs = []
    for x, y, z, c in every():
        if (c == 0) != swapped:
            pairs.append((ident(x, y, z, c), ident(x + step, y, z, c)))
        else:
            pairs.append((ident(x, y, z, c), ident(x, y + step, z, c)))
    return lax.ppermute(value, AX, pairs)


def shift_g(value, step):
    return shift_plane(value, step, False)


def shift_p(value, step):
    return shift_plane(value, step, True)


def swap_core(value):
    return lax.ppermute(value, AX, [(ident(x, y, z, c), ident(x, y, z, 1 - c)) for x, y, z, c in every()])


def cost(flops, moved):
    return pl.CostEstimate(flops=flops, bytes_accessed=moved, transcendentals=0)


def cycle_kernel(place, cyc_map, cyc, out):
    core, column = place[2], place[3]
    tiles = HALF // TB
    shares = []
    for share in range(4):
        cut = []
        for t in range(share * 16, share * 16 + 16):
            keep = cyc_map[core * tiles + t, column].astype(F32)
            cut.append((cyc[:, t * TB : (t + 1) * TB].astype(F32) * keep))
        shares.append(jnp.concatenate(cut, 1))
    first = core == 0
    for i in range(4):
        for j in range(0, 4, 2):
            top = jnp.where(first, shares[i], shares[j])
            low = jnp.where(first, shares[i], shares[j + 1])
            at = (i * 4 + j) * WD
            out[at : at + 2 * WD, :] = jnp.concatenate([top, low], 0).astype(BF)


def cycle_shares(place, cycle_map, cyc):
    return pl.pallas_call(
        cycle_kernel,
        out_shape=jax.ShapeDtypeStruct((16 * WD, PART), BF),
        grid_spec=pltpu.PrefetchScalarGridSpec(
            num_scalar_prefetch=2, grid=(), in_specs=[VMEM], out_specs=VMEM
        ),
        compiler_params=PARAMS,
        cost_estimate=cost(0, 700_000),
    )(place, cycle_map, cyc)


def amp_kernel(place, amp_map, *refs):
    ins, outs, win = refs[:4], refs[4:8], refs[8]
    step = pl.program_id(0)
    for d in range(4):
        share = lax.rem(place[0] + d, 4)
        for t in range(PART // TB):
            keep = amp_map[0, share * 16 + t].astype(BF)
            outs[d][:, t * TB : (t + 1) * TB] = ins[d][:, t * TB : (t + 1) * TB] * keep

        @pl.when(step == 0)
        def _():
            win[:, pl.ds(pl.multiple_of(share * PART, PART), PART)] = outs[d][:16, :]


def amp_shares(place, amp_map, amplitudes):
    block = 32

    def source(d):
        return pl.BlockSpec((block, PART), lambda i, place, amp_map: (i, lax.rem(place[0] + d, 4)))

    return pl.pallas_call(
        amp_kernel,
        out_shape=[jax.ShapeDtypeStruct((ROWS, PART), BF)] * 4 + [jax.ShapeDtypeStruct((16, HALF), BF)],
        grid_spec=pltpu.PrefetchScalarGridSpec(
            num_scalar_prefetch=2,
            grid=(ROWS // block,),
            in_specs=[source(d) for d in range(4)],
            out_specs=[pl.BlockSpec((block, PART), lambda i, place, amp_map: (i, 0))] * 4
            + [pl.BlockSpec((16, HALF), lambda i, place, amp_map: (0, 0))],
        ),
        compiler_params=PARAMS,
        cost_estimate=cost(0, 4_000_000),
    )(place, amp_map, *[amplitudes] * 4)


def dressed_kernel(first, count, *refs):
    blocks, cyc = refs[:4], refs[4 : 4 + count]
    away, own = refs[-2:]
    left = jnp.concatenate([blocks[d][...] for d in (1, 2, 3, 0)], 0)
    for at in range(0, count, 2):
        right = jnp.concatenate([ref[...] for ref in cyc[at : at + 2]], 0)
        wide = right.shape[0]
        value = lax.dot_general(left, right, (((1,), (1,)), ((), ())), preferred_element_type=F32)
        where = slice(first + at * 128, first + at * 128 + wide)
        away[:, where] = value[: 3 * ROWS].astype(BF)
        own[:, where] = value[3 * ROWS :]


def dressed_first(blocks, cyc):
    return pl.pallas_call(
        functools.partial(dressed_kernel, 0, len(cyc)),
        out_shape=[jax.ShapeDtypeStruct((3 * ROWS, QW), BF), jax.ShapeDtypeStruct((ROWS, QW), F32)],
        in_specs=[VMEM] * (4 + len(cyc)),
        out_specs=[VMEM] * 2,
        compiler_params=PARAMS,
        cost_estimate=cost(2 * 512 * PART * 896, 8_000_000),
    )(*blocks, *cyc)


def dressed_last_kernel(*refs):
    blocks, halves, away_in, own_in = refs[:4], refs[4:6], refs[6], refs[7]
    outs, own = refs[8:11], refs[11]
    edge = 7 * 128
    left = jnp.concatenate([blocks[d][...] for d in (1, 2, 3, 0)], 0)
    right = jnp.concatenate([ref[...] for ref in halves], 0)
    value = lax.dot_general(left, right, (((1,), (1,)), ((), ())), preferred_element_type=F32)
    for d in range(3):
        rows = slice(d * ROWS, (d + 1) * ROWS)
        outs[d][:, :edge] = away_in[rows, :edge]
        outs[d][:, edge:] = value[rows].astype(BF)
    own[:, :edge] = own_in[:, :edge]
    own[:, edge:] = value[3 * ROWS :]


def dressed_last(blocks, halves, away, own):
    return pl.pallas_call(
        dressed_last_kernel,
        out_shape=[jax.ShapeDtypeStruct((ROWS, QW), BF)] * 3 + [jax.ShapeDtypeStruct((ROWS, QW), F32)],
        in_specs=[VMEM] * 8,
        out_specs=[VMEM] * 4,
        compiler_params=PARAMS,
        cost_estimate=cost(2 * 512 * PART * 128, 5_000_000),
    )(*blocks, *halves, away, own)


def window_cut_kernel(place, *refs):
    pieces, outs = refs[:8], refs[8:]
    for d in range(4):
        share = pl.ds(pl.multiple_of(lax.rem(place[0] + 4 - d, 4) * PART, PART), PART)
        for m in range(0, 8, 2):
            pair = jnp.concatenate([pieces[m][:, share], pieces[m + 1][:, share]], 0)
            outs[d][m * WD : (m + 2) * WD, :] = pair


def window_cut(place, pieces):
    return pl.pallas_call(
        window_cut_kernel,
        out_shape=[jax.ShapeDtypeStruct((NZ * WD, PART), BF)] * 4,
        grid_spec=pltpu.PrefetchScalarGridSpec(
            num_scalar_prefetch=1, grid=(), in_specs=[VMEM] * 8, out_specs=[VMEM] * 4
        ),
        compiler_params=PARAMS,
        cost_estimate=cost(0, 2_000_000),
    )(place, *pieces)


def window_order_kernel(place, *refs):
    pieces, out = refs[:4], refs[4]
    for d in range(4):
        at = pl.multiple_of(lax.rem(place[0] + d, 4) * NZ * WD, NZ * WD)
        out[pl.ds(at, NZ * WD), :] = pieces[d][...]


def window_order(place, pieces):
    return pl.pallas_call(
        window_order_kernel,
        out_shape=jax.ShapeDtypeStruct((4 * NZ * WD, PART), BF),
        grid_spec=pltpu.PrefetchScalarGridSpec(
            num_scalar_prefetch=1, grid=(), in_specs=[VMEM] * 4, out_specs=VMEM
        ),
        compiler_params=PARAMS,
        cost_estimate=cost(0, 2_000_000),
    )(place, *pieces)


def inner_kernel(mine, other, order, full, inner):
    value = (mine[...] + other[...]).astype(BF)
    full[...] = value
    inner[...] = jnp.dot(value, order[...], preferred_element_type=F32).astype(BF)


def inner_call(mine, other, order):
    return pl.pallas_call(
        inner_kernel,
        out_shape=[jax.ShapeDtypeStruct((ROWS, QW), BF)] * 2,
        in_specs=[VMEM] * 3,
        out_specs=[VMEM] * 2,
        compiler_params=PARAMS,
        cost_estimate=cost(2 * ROWS * QW * QW, 4_000_000),
    )(mine, other, order)


def quadratic_kernel(count, *refs):
    lefts, rights, outs = refs[:count], refs[count : count + 5], refs[count + 5 :]
    left = jnp.concatenate([ref[...] for ref in lefts], 0)
    wide = 512
    for n in range(0, PART, wide):
        right = jnp.concatenate([ref[:, n : n + wide] for ref in rights], 0)
        value = jnp.dot(left, right, preferred_element_type=F32).astype(BF)
        for d in range(count):
            outs[d][:, n : n + wide] = value[d * ROWS : (d + 1) * ROWS]


def quadratic_blocks(lefts, rights):
    count = len(lefts)
    return pl.pallas_call(
        functools.partial(quadratic_kernel, count),
        out_shape=[jax.ShapeDtypeStruct((ROWS, PART), BF)] * count,
        in_specs=[VMEM] * (count + 5),
        out_specs=[VMEM] * count,
        compiler_params=PARAMS,
        cost_estimate=cost(2 * count * ROWS * QW * PART, 5_000_000),
    )(*lefts, *rights)


def place_kernel(place, *refs):
    ins, out, sem = refs[:4], refs[4], refs[5]
    copies = []
    for d in range(4):
        at = pl.multiple_of(lax.rem(place[0] + d, 4) * PART, PART)
        copies.append(pltpu.make_async_copy(ins[d], out.at[:, pl.ds(at, PART)], sem.at[d]))
    for copy in copies:
        copy.start()
    for copy in copies:
        copy.wait()


def place_blocks(place, blocks):
    anywhere = pl.BlockSpec(memory_space=pl.ANY)
    return pl.pallas_call(
        place_kernel,
        out_shape=jax.ShapeDtypeStruct((ROWS, HALF), BF),
        grid_spec=pltpu.PrefetchScalarGridSpec(
            num_scalar_prefetch=1,
            grid=(),
            in_specs=[anywhere] * 4,
            out_specs=anywhere,
            scratch_shapes=[pltpu.SemaphoreType.DMA((4,))],
        ),
        compiler_params=PARAMS,
        cost_estimate=cost(0, 4_000_000),
    )(place, *blocks)


def body(amplitudes, cycle_integrals, amp_map, cycle_map):
    row, col, core = (lax.axis_index(a) for a in AX)
    x, y, z = row, col // NZ, col % NZ
    g = jnp.where(core == 0, x, y)
    p = jnp.where(core == 0, y, x)
    place = jnp.stack([g, p, core, row * NY * NZ + col]).astype(jnp.int32)

    cyc = cycle_shares(place, cycle_map, cycle_integrals.T)
    plane = [[i * NY * NZ + j * NZ + k for i in range(NX) for j in range(NY)] for k in range(NZ)]
    cyc = lax.all_to_all(cyc, ("row", "col"), 0, 0, tiled=True, axis_index_groups=plane)
    cf, cb = shift_z(cyc, 1), shift_z(cyc, -1)
    cf2, cb2 = shift_z(cf, 1), shift_z(cb, -1)
    cf3, cb3 = shift_z(cf2, 1), shift_z(cb2, -1)
    middle = cyc.shape[0] // 2
    far = [shift_z(cb3[:middle], -1), shift_z(cf3[middle:], 1)]

    *sends, win = amp_shares(place, amp_map, amplitudes)
    blocks = [sends[0]] + [shift_g(sends[d], d) for d in (1, 2, 3)]

    win = win[:WD]
    f, b = shift_z(win, 1), shift_z(win, -1)
    f2, b2 = shift_z(f, 1), shift_z(b, -1)
    f3, b3 = shift_z(f2, 1), shift_z(b2, -1)
    b4 = shift_z(b3, -1)
    cuts = window_cut(place, [win, b, b2, b3, b4, f3, f2, f])
    win = window_order(place, [cuts[0]] + [shift_g(cuts[d], -d) for d in (1, 2, 3)])
    wf, wb = shift_p(win, 1), shift_p(win, -1)
    rows = win.shape[0] // 2
    rights = [win, wb, shift_p(wb[:rows], -1), shift_p(wf[rows:], 1), wf]

    here = lax.broadcasted_iota(jnp.int32, (QW, 1), 0)
    turn = here // 128
    hz = (z + jnp.where(turn % 2 == 1, (turn + 1) // 2, 8 - turn // 2)) % NZ
    hx, hy, hw = here // 32 % 4, here // 8 % 4, here % 8
    hg, hp = jnp.where(core == 0, hx, hy), jnp.where(core == 0, hy, hx)
    there = lax.broadcasted_iota(jnp.int32, (1, QW), 1)
    order = ((hp - p) % 4 * 256 + hg * 64 + (hz - z) % NZ * 8 + hw == there).astype(BF)
    there = lax.broadcasted_iota(jnp.int32, (1, QW // 2), 1) + core * (QW // 2)
    output_order = (hx * 256 + hy * 64 + hz * 8 + hw == there).astype(BF)

    away, own = dressed_first(blocks, [cyc, cb, cf, cb2, cf2, cb3, cf3])
    *away, total = dressed_last(blocks, far, away, own)
    back = [shift_g(away[d - 1], -d) for d in (1, 2, 3)]
    for value in back:
        total = total + value.astype(F32)
    full, inner = inner_call(total, swap_core(total), order)
    dressed = jnp.dot(full, output_order, preferred_element_type=F32).astype(BF)

    inners = [shift_g(inner, d) for d in (1, 2, 3)]
    outs = quadratic_blocks(inners, rights)
    outs = [shift_g(outs[d - 1], -d) for d in (1, 2, 3)]
    outs = list(quadratic_blocks([inner], rights)) + outs
    return (dressed, place_blocks(place, outs))


def solution(mesh):
    placed = (P(("row", "col"), "rep"), P("rep", ("row", "col")), P(("row", "col"), "rep"), P())
    return jax.shard_map(
        body,
        mesh=mesh,
        in_specs=placed,
        out_specs=(P(("row", "col"), "rep"), P(("row", "col"), "rep")),
        check_vma=False,
    )
```

```python
import functools

import jax
import jax.numpy as jnp
from jax import lax
from jax.experimental import pallas as pl
from jax.experimental.pallas import tpu as pltpu
from jax.sharding import PartitionSpec as P

TB = 128
WD = 8
NX, NY, NZ = 4, 4, 8
AX = ("row", "col", "rep")
F32, BF = jnp.float32, jnp.bfloat16
ROWS = 128
HALF = 8192
PART = HALF // 4
QW = 1024
VMEM = pl.BlockSpec(memory_space=pltpu.VMEM)
PARAMS = pltpu.CompilerParams(vmem_limit_bytes=40 * 2**20)


def ident(x, y, z, c):
    return ((x % NX) * NY * NZ + (y % NY) * NZ + z % NZ) * 2 + c


def every():
    return [(x, y, z, c) for x in range(NX) for y in range(NY) for z in range(NZ) for c in (0, 1)]


def shift_z(value, step):
    return lax.ppermute(value, AX, [(ident(x, y, z, c), ident(x, y, z + step, c)) for x, y, z, c in every()])


def shift_plane(value, step, swapped):
    pairs = []
    for x, y, z, c in every():
        if (c == 0) != swapped:
            pairs.append((ident(x, y, z, c), ident(x + step, y, z, c)))
        else:
            pairs.append((ident(x, y, z, c), ident(x, y + step, z, c)))
    return lax.ppermute(value, AX, pairs)


def shift_g(value, step):
    return shift_plane(value, step, False)


def shift_p(value, step):
    return shift_plane(value, step, True)


def swap_core(value):
    return lax.ppermute(value, AX, [(ident(x, y, z, c), ident(x, y, z, 1 - c)) for x, y, z, c in every()])


def cost(flops, moved):
    return pl.CostEstimate(flops=flops, bytes_accessed=moved, transcendentals=0)


def cycle_kernel(place, cyc_map, cyc, *outs):
    core, column = place[2], place[3]
    tiles = HALF // TB
    for d in range(4):
        share = lax.rem(place[0] + d, 4)
        for t in range(PART // TB):
            keep = cyc_map[core * tiles + share * 16 + t, column].astype(F32)
            at = pl.multiple_of(share * PART + t * TB, TB)
            outs[d][:, t * TB : (t + 1) * TB] = (cyc[:, pl.ds(at, TB)].astype(F32) * keep).astype(BF)


def cycle_shares(place, cycle_map, cyc):
    return pl.pallas_call(
        cycle_kernel,
        out_shape=[jax.ShapeDtypeStruct((WD, PART), BF)] * 4,
        grid_spec=pltpu.PrefetchScalarGridSpec(
            num_scalar_prefetch=2, grid=(), in_specs=[VMEM], out_specs=[VMEM] * 4
        ),
        compiler_params=PARAMS,
        cost_estimate=cost(0, 300_000),
    )(place, cycle_map, cyc)


def stack_kernel(*refs):
    refs[4][...] = jnp.concatenate([ref[...] for ref in refs[:4]], 0)


def stack(pieces):
    return pl.pallas_call(
        stack_kernel,
        out_shape=jax.ShapeDtypeStruct((4 * pieces[0].shape[0], PART), BF),
        in_specs=[VMEM] * 4,
        out_specs=VMEM,
        compiler_params=PARAMS,
        cost_estimate=cost(0, 300_000),
    )(*pieces)


def plane_kernel(place, *refs):
    pieces, out = refs[:4], refs[4]
    rows = 16 * WD
    here = lax.broadcasted_iota(jnp.int32, (rows, rows), 1)
    there = lax.broadcasted_iota(jnp.int32, (rows, rows), 0)
    hp, hg, hw = (here // 32 + place[1]) % 4, (here // 8 + place[0]) % 4, here % 8
    first = place[2] == 0
    at = jnp.where(first, hg * 32 + hp * 8, hp * 32 + hg * 8) + hw
    order = (at == there).astype(F32).astype(BF)
    value = jnp.concatenate([ref[...] for ref in pieces], 0)
    out[...] = jnp.dot(order, value, preferred_element_type=F32).astype(BF)


def plane_order(place, pieces):
    return pl.pallas_call(
        plane_kernel,
        out_shape=jax.ShapeDtypeStruct((16 * WD, PART), BF),
        grid_spec=pltpu.PrefetchScalarGridSpec(
            num_scalar_prefetch=1, grid=(), in_specs=[VMEM] * 4, out_specs=VMEM
        ),
        compiler_params=PARAMS,
        cost_estimate=cost(2 * 128 * 128 * PART, 1_000_000),
    )(place, *pieces)


def amp_kernel(place, amp_map, *refs):
    ins, outs, win = refs[:4], refs[4:8], refs[8]
    step = pl.program_id(0)
    for d in range(4):
        share = lax.rem(place[0] + d, 4)
        for t in range(PART // TB):
            keep = amp_map[0, share * 16 + t].astype(BF)
            outs[d][:, t * TB : (t + 1) * TB] = ins[d][:, t * TB : (t + 1) * TB] * keep

        @pl.when(step == 0)
        def _():
            win[:, pl.ds(pl.multiple_of(share * PART, PART), PART)] = outs[d][:16, :]


def amp_shares(place, amp_map, amplitudes):
    block = 32

    def source(d):
        return pl.BlockSpec((block, PART), lambda i, place, amp_map: (i, lax.rem(place[0] + d, 4)))

    return pl.pallas_call(
        amp_kernel,
        out_shape=[jax.ShapeDtypeStruct((ROWS, PART), BF)] * 4 + [jax.ShapeDtypeStruct((16, HALF), BF)],
        grid_spec=pltpu.PrefetchScalarGridSpec(
            num_scalar_prefetch=2,
            grid=(ROWS // block,),
            in_specs=[source(d) for d in range(4)],
            out_specs=[pl.BlockSpec((block, PART), lambda i, place, amp_map: (i, 0))] * 4
            + [pl.BlockSpec((16, HALF), lambda i, place, amp_map: (0, 0))],
        ),
        compiler_params=PARAMS,
        cost_estimate=cost(0, 4_000_000),
    )(place, amp_map, *[amplitudes] * 4)


def dressed_kernel(first, count, *refs):
    blocks, cyc = refs[:4], refs[4 : 4 + count]
    away, own = refs[-2:]
    left = jnp.concatenate([blocks[d][...] for d in (1, 2, 3, 0)], 0)
    for at in range(0, count, 2):
        right = jnp.concatenate([ref[...] for ref in cyc[at : at + 2]], 0)
        wide = right.shape[0]
        value = lax.dot_general(left, right, (((1,), (1,)), ((), ())), preferred_element_type=F32)
        where = slice(first + at * 128, first + at * 128 + wide)
        away[:, where] = value[: 3 * ROWS].astype(BF)
        own[:, where] = value[3 * ROWS :]


def dressed_first(blocks, cyc):
    return pl.pallas_call(
        functools.partial(dressed_kernel, 0, len(cyc)),
        out_shape=[jax.ShapeDtypeStruct((3 * ROWS, QW), BF), jax.ShapeDtypeStruct((ROWS, QW), F32)],
        in_specs=[VMEM] * (4 + len(cyc)),
        out_specs=[VMEM] * 2,
        compiler_params=PARAMS,
        cost_estimate=cost(2 * 512 * PART * 896, 8_000_000),
    )(*blocks, *cyc)


def dressed_last_kernel(*refs):
    blocks, halves, away_in, own_in = refs[:4], refs[4:6], refs[6], refs[7]
    outs, own = refs[8:11], refs[11]
    edge = 7 * 128
    left = jnp.concatenate([blocks[d][...] for d in (1, 2, 3, 0)], 0)
    right = jnp.concatenate([ref[...] for ref in halves], 0)
    value = lax.dot_general(left, right, (((1,), (1,)), ((), ())), preferred_element_type=F32)
    for d in range(3):
        rows = slice(d * ROWS, (d + 1) * ROWS)
        outs[d][:, :edge] = away_in[rows, :edge]
        outs[d][:, edge:] = value[rows].astype(BF)
    own[:, :edge] = own_in[:, :edge]
    own[:, edge:] = value[3 * ROWS :]


def dressed_last(blocks, halves, away, own):
    return pl.pallas_call(
        dressed_last_kernel,
        out_shape=[jax.ShapeDtypeStruct((ROWS, QW), BF)] * 3 + [jax.ShapeDtypeStruct((ROWS, QW), F32)],
        in_specs=[VMEM] * 8,
        out_specs=[VMEM] * 4,
        compiler_params=PARAMS,
        cost_estimate=cost(2 * 512 * PART * 128, 5_000_000),
    )(*blocks, *halves, away, own)


def window_cut_kernel(place, *refs):
    pieces, outs = refs[:8], refs[8:]
    for d in range(4):
        share = pl.ds(pl.multiple_of(lax.rem(place[0] + 4 - d, 4) * PART, PART), PART)
        for m in range(0, 8, 2):
            pair = jnp.concatenate([pieces[m][:, share], pieces[m + 1][:, share]], 0)
            outs[d][m * WD : (m + 2) * WD, :] = pair


def window_cut(place, pieces):
    return pl.pallas_call(
        window_cut_kernel,
        out_shape=[jax.ShapeDtypeStruct((NZ * WD, PART), BF)] * 4,
        grid_spec=pltpu.PrefetchScalarGridSpec(
            num_scalar_prefetch=1, grid=(), in_specs=[VMEM] * 8, out_specs=[VMEM] * 4
        ),
        compiler_params=PARAMS,
        cost_estimate=cost(0, 2_000_000),
    )(place, *pieces)


def window_order_kernel(place, *refs):
    pieces, out = refs[:4], refs[4]
    for d in range(4):
        at = pl.multiple_of(lax.rem(place[0] + d, 4) * NZ * WD, NZ * WD)
        out[pl.ds(at, NZ * WD), :] = pieces[d][...]


def window_order(place, pieces):
    return pl.pallas_call(
        window_order_kernel,
        out_shape=jax.ShapeDtypeStruct((4 * NZ * WD, PART), BF),
        grid_spec=pltpu.PrefetchScalarGridSpec(
            num_scalar_prefetch=1, grid=(), in_specs=[VMEM] * 4, out_specs=VMEM
        ),
        compiler_params=PARAMS,
        cost_estimate=cost(0, 2_000_000),
    )(place, *pieces)


def inner_kernel(mine, other, order, full, inner):
    value = (mine[...] + other[...]).astype(BF)
    full[...] = value
    inner[...] = jnp.dot(value, order[...], preferred_element_type=F32).astype(BF)


def inner_call(mine, other, order):
    return pl.pallas_call(
        inner_kernel,
        out_shape=[jax.ShapeDtypeStruct((ROWS, QW), BF)] * 2,
        in_specs=[VMEM] * 3,
        out_specs=[VMEM] * 2,
        compiler_params=PARAMS,
        cost_estimate=cost(2 * ROWS * QW * QW, 4_000_000),
    )(mine, other, order)


def quadratic_kernel(count, *refs):
    lefts, rights, outs = refs[:count], refs[count : count + 5], refs[count + 5 :]
    left = jnp.concatenate([ref[...] for ref in lefts], 0)
    wide = 512
    for n in range(0, PART, wide):
        right = jnp.concatenate([ref[:, n : n + wide] for ref in rights], 0)
        value = jnp.dot(left, right, preferred_element_type=F32).astype(BF)
        for d in range(count):
            outs[d][:, n : n + wide] = value[d * ROWS : (d + 1) * ROWS]


def quadratic_blocks(lefts, rights):
    count = len(lefts)
    return pl.pallas_call(
        functools.partial(quadratic_kernel, count),
        out_shape=[jax.ShapeDtypeStruct((ROWS, PART), BF)] * count,
        in_specs=[VMEM] * (count + 5),
        out_specs=[VMEM] * count,
        compiler_params=PARAMS,
        cost_estimate=cost(2 * count * ROWS * QW * PART, 5_000_000),
    )(*lefts, *rights)


def place_kernel(place, *refs):
    ins, out = refs[:4], refs[4]
    for d in range(4):
        at = pl.multiple_of(lax.rem(place[0] + d, 4) * PART, PART)
        out[:, pl.ds(at, PART)] = ins[d][...]


def place_blocks(place, blocks):
    block = 32
    return pl.pallas_call(
        place_kernel,
        out_shape=jax.ShapeDtypeStruct((ROWS, HALF), BF),
        grid_spec=pltpu.PrefetchScalarGridSpec(
            num_scalar_prefetch=1,
            grid=(ROWS // block,),
            in_specs=[pl.BlockSpec((block, PART), lambda i, place: (i, 0))] * 4,
            out_specs=pl.BlockSpec((block, HALF), lambda i, place: (i, 0)),
        ),
        compiler_params=PARAMS,
        cost_estimate=cost(0, 4_000_000),
    )(place, *blocks)


def after(values, *others):
    count = len(values)
    return lax.optimization_barrier(tuple(values) + others)[:count]


def body(amplitudes, cycle_integrals, amp_map, cycle_map):
    row, col, core = (lax.axis_index(a) for a in AX)
    x, y, z = row, col // NZ, col % NZ
    g = jnp.where(core == 0, x, y)
    p = jnp.where(core == 0, y, x)
    place = jnp.stack([g, p, core, row * NY * NZ + col]).astype(jnp.int32)

    shares = cycle_shares(place, cycle_map, cycle_integrals.T)
    shares = [shares[0]] + [shift_g(shares[4 - d], -d) for d in (1, 2, 3)]
    *sends, win = amp_shares(place, amp_map, amplitudes)
    win = win[:WD]
    cyc = stack(after(shares, win))
    sends[1:2] = after(sends[1:2], cyc)
    block1 = shift_g(sends[1], 1)
    wf, wb = shift_z(win, 1), shift_z(win, -1)
    cyc = plane_order(place, after([cyc] + [shift_p(cyc, -e) for e in (1, 2, 3)], wf, wb))

    cf, cb = shift_z(cyc, 1), shift_z(cyc, -1)
    wf, wb, sends[3] = after([wf, wb, sends[3]], cyc)
    wf2, wb2 = shift_z(wf, 1), shift_z(wb, -1)
    block3 = shift_g(sends[3], 3)
    wf3, wb3 = shift_z(wf2, 1), shift_z(wb2, -1)
    cf, cb, wb3, sends[2], block1 = after([cf, cb, wb3, sends[2], block1], wf3)

    cf2, cb2 = shift_z(cf, 1), shift_z(cb, -1)
    wb4 = shift_z(wb3, -1)
    block2 = shift_g(sends[2], 2)
    cuts = window_cut(place, [win, wb, wb2, wb3, wb4, wf3, wf2, wf])
    cf2, cb2, block3, *cuts = after([cf2, cb2, block3, *cuts])

    cf3, cb3 = shift_z(cf2, 1), shift_z(cb2, -1)
    win = window_order(place, [cuts[0]] + [shift_g(cuts[d], -d) for d in (1, 2, 3)])
    cf3, cb3, block2, win = after([cf3, cb3, block2, win])

    middle = cyc.shape[0] // 2
    far = [shift_z(cb3[:middle], -1), shift_z(cf3[middle:], 1)]
    wf, wb = shift_p(win, 1), shift_p(win, -1)
    blocks = [sends[0], block1, block2, block3]

    here = lax.broadcasted_iota(jnp.int32, (QW, 1), 0)
    turn = here // 128
    hz = (z + jnp.where(turn % 2 == 1, (turn + 1) // 2, 8 - turn // 2)) % NZ
    hx, hy, hw = here // 32 % 4, here // 8 % 4, here % 8
    hg, hp = jnp.where(core == 0, hx, hy), jnp.where(core == 0, hy, hx)
    there = lax.broadcasted_iota(jnp.int32, (1, QW), 1)
    order = ((hp - p) % 4 * 256 + hg * 64 + (hz - z) % NZ * 8 + hw == there).astype(BF)
    there = lax.broadcasted_iota(jnp.int32, (1, QW // 2), 1) + core * (QW // 2)
    output_order = (hx * 256 + hy * 64 + hz * 8 + hw == there).astype(BF)

    away, own = dressed_first(blocks, [cyc, cb, cf, cb2, cf2, cb3, cf3])
    *away, total = dressed_last(blocks, far, away, own)
    back = [shift_g(away[d - 1], -d) for d in (1, 2, 3)]
    wf, wb, *back = after([wf, wb, *back])
    for value in back:
        total = total + value.astype(F32)
    other = swap_core(total)
    rows = win.shape[0] // 2
    rights = [win, wb, shift_p(wb[:rows], -1), shift_p(wf[rows:], 1), wf]
    full, inner = inner_call(total, other, order)
    dressed = jnp.dot(full, output_order, preferred_element_type=F32).astype(BF)

    inners = [shift_g(inner, d) for d in (1, 2, 3)]
    outs = quadratic_blocks(inners, rights)
    outs = [shift_g(outs[d - 1], -d) for d in (1, 2, 3)]
    outs = list(quadratic_blocks([inner], rights)) + outs
    return (dressed, place_blocks(place, outs))


def solution(mesh):
    placed = (P(("row", "col"), "rep"), P("rep", ("row", "col")), P(("row", "col"), "rep"), P())
    return jax.shard_map(
        body,
        mesh=mesh,
        in_specs=placed,
        out_specs=(P(("row", "col"), "rep"), P(("row", "col"), "rep")),
        check_vma=False,
    )
```

```python
import functools

import jax
import jax.numpy as jnp
from jax import lax
from jax.experimental import pallas as pl
from jax.experimental.pallas import tpu as pltpu
from jax.sharding import PartitionSpec as P

TB = 128
WD = 8
NX, NY, NZ = 4, 4, 8
AX = ("row", "col", "rep")
F32, BF = jnp.float32, jnp.bfloat16
ROWS = 128
HALF = 8192
PART = HALF // 4
QW = 1024
VMEM = pl.BlockSpec(memory_space=pltpu.VMEM)
PARAMS = pltpu.CompilerParams(vmem_limit_bytes=40 * 2**20)


def ident(x, y, z, c):
    return ((x % NX) * NY * NZ + (y % NY) * NZ + z % NZ) * 2 + c


def every():
    return [(x, y, z, c) for x in range(NX) for y in range(NY) for z in range(NZ) for c in (0, 1)]


def shift_z(value, step):
    return lax.ppermute(value, AX, [(ident(x, y, z, c), ident(x, y, z + step, c)) for x, y, z, c in every()])


def shift_plane(value, step, swapped):
    pairs = []
    for x, y, z, c in every():
        if (c == 0) != swapped:
            pairs.append((ident(x, y, z, c), ident(x + step, y, z, c)))
        else:
            pairs.append((ident(x, y, z, c), ident(x, y + step, z, c)))
    return lax.ppermute(value, AX, pairs)


def shift_g(value, step):
    return shift_plane(value, step, False)


def shift_p(value, step):
    return shift_plane(value, step, True)


def swap_core(value):
    return lax.ppermute(value, AX, [(ident(x, y, z, c), ident(x, y, z, 1 - c)) for x, y, z, c in every()])


def cost(flops, moved):
    return pl.CostEstimate(flops=flops, bytes_accessed=moved, transcendentals=0)


def shares_kernel(cyc_map, amp_map, cyc, amp, *refs):
    outs, rows, both, sem = refs[:4], refs[4], refs[5], refs[6]
    row, col, core = (lax.axis_index(a) for a in AX)
    g = jnp.where(core == 0, row, col // NZ)
    copy = pltpu.make_async_copy(amp.at[0:16, :], rows, sem)
    copy.start()
    tiles = HALF // TB
    half_map = cyc_map[pl.ds(pl.multiple_of(core * tiles, tiles), tiles), :].astype(F32)
    lane = lax.broadcasted_iota(jnp.int32, half_map.shape, 1)
    keep = jnp.sum(jnp.where(lane == row * NY * NZ + col, half_map, 0.0), axis=1, keepdims=True)
    keep_window = amp_map[...].astype(F32)
    copy.wait()
    for t in range(tiles):
        at = slice(t * TB, (t + 1) * TB)
        top = cyc[:, at].astype(F32) * keep[t : t + 1, :]
        low = rows[:WD, at].astype(F32) * keep_window[:, t : t + 1]
        both[:, at] = jnp.concatenate([top, low], 0).astype(BF)
    for d in range(4):
        share = pl.multiple_of(lax.rem(g + d, 4) * PART, PART)
        outs[d][...] = both[:, pl.ds(share, PART)]


def small_shares(cycle_map, amp_map, cyc, amplitudes):
    return pl.pallas_call(
        shares_kernel,
        out_shape=[jax.ShapeDtypeStruct((2 * WD, PART), BF)] * 4,
        in_specs=[VMEM] * 3 + [pl.BlockSpec(memory_space=pl.ANY)],
        out_specs=[VMEM] * 4,
        scratch_shapes=[
            pltpu.VMEM((16, HALF), BF),
            pltpu.VMEM((16, HALF), BF),
            pltpu.SemaphoreType.DMA,
        ],
        compiler_params=pltpu.CompilerParams(vmem_limit_bytes=60 * 2**20),
        cost_estimate=cost(0, 600_000),
    )(cycle_map, amp_map, cyc, amplitudes)


def group_kernel(place, *refs):
    pieces, outs = refs[:4], refs[4:]
    rows = 8 * WD
    here = lax.broadcasted_iota(jnp.int32, (rows, rows), 1)
    there = lax.broadcasted_iota(jnp.int32, (rows, rows), 0)
    member = jnp.where(here // 8 % 2 == 0, (here // 16 + place[0]) % 4, 4 + here // 16)
    order = (member * 8 + here % 8 == there).astype(F32).astype(BF)
    value = jnp.concatenate([ref[...] for ref in pieces], 0)
    value = jnp.dot(order, value, preferred_element_type=F32).astype(BF)
    outs[0][...] = value[: rows // 2]
    outs[1][...] = value[rows // 2 :]


def group_order(place, pieces):
    return pl.pallas_call(
        group_kernel,
        out_shape=[jax.ShapeDtypeStruct((4 * WD, PART), BF)] * 2,
        grid_spec=pltpu.PrefetchScalarGridSpec(
            num_scalar_prefetch=1, grid=(), in_specs=[VMEM] * 4, out_specs=[VMEM] * 2
        ),
        compiler_params=PARAMS,
        cost_estimate=cost(2 * 64 * 64 * PART, 600_000),
    )(place, *pieces)


def stack_kernel(*refs):
    refs[-1][...] = jnp.concatenate([ref[...] for ref in refs[:-1]], 0)


def stack(pieces):
    return pl.pallas_call(
        stack_kernel,
        out_shape=jax.ShapeDtypeStruct((sum(piece.shape[0] for piece in pieces), PART), BF),
        in_specs=[VMEM] * len(pieces),
        out_specs=VMEM,
        compiler_params=PARAMS,
        cost_estimate=cost(0, 2_000_000),
    )(*pieces)


def plane_kernel(place, *refs):
    pieces, out = refs[:4], refs[4]
    rows = 16 * WD
    here = lax.broadcasted_iota(jnp.int32, (rows, rows), 1)
    there = lax.broadcasted_iota(jnp.int32, (rows, rows), 0)
    hp, hg, hw = (here // 32 + place[1]) % 4, (here // 8 + place[0]) % 4, here % 8
    first = place[2] == 0
    at = jnp.where(first, hg * 32 + hp * 8, hp * 32 + hg * 8) + hw
    order = (at == there).astype(F32).astype(BF)
    value = jnp.concatenate([ref[...] for ref in pieces], 0)
    out[...] = jnp.dot(order, value, preferred_element_type=F32).astype(BF)


def plane_order(place, pieces):
    return pl.pallas_call(
        plane_kernel,
        out_shape=jax.ShapeDtypeStruct((16 * WD, PART), BF),
        grid_spec=pltpu.PrefetchScalarGridSpec(
            num_scalar_prefetch=1, grid=(), in_specs=[VMEM] * 4, out_specs=VMEM
        ),
        compiler_params=PARAMS,
        cost_estimate=cost(2 * 128 * 128 * PART, 1_000_000),
    )(place, *pieces)


def amp_kernel(place, amp_map, *refs):
    ins, outs = refs[:4], refs[4:]
    for d in range(4):
        share = lax.rem(place[0] + d, 4)
        for t in range(PART // TB):
            keep = amp_map[0, share * 16 + t].astype(BF)
            outs[d][:, t * TB : (t + 1) * TB] = ins[d][:, t * TB : (t + 1) * TB] * keep


def amp_shares(place, amp_map, amplitudes):
    block = 32

    def source(d):
        return pl.BlockSpec((block, PART), lambda i, place, amp_map: (i, lax.rem(place[0] + d, 4)))

    return pl.pallas_call(
        amp_kernel,
        out_shape=[jax.ShapeDtypeStruct((ROWS, PART), BF)] * 4,
        grid_spec=pltpu.PrefetchScalarGridSpec(
            num_scalar_prefetch=2,
            grid=(ROWS // block,),
            in_specs=[source(d) for d in range(4)],
            out_specs=[pl.BlockSpec((block, PART), lambda i, place, amp_map: (i, 0))] * 4,
        ),
        compiler_params=PARAMS,
        cost_estimate=cost(0, 4_000_000),
    )(place, amp_map, *[amplitudes] * 4)


def dressed_kernel(count, *refs):
    blocks, cyc = refs[:4], refs[4 : 4 + count]
    away, own = refs[-2:]
    left = jnp.concatenate([blocks[d][...] for d in (1, 2, 3, 0)], 0)
    for at in range(count):
        value = lax.dot_general(left, cyc[at][...], (((1,), (1,)), ((), ())), preferred_element_type=F32)
        where = slice(at * 256, at * 256 + 256)
        away[:, where] = value[: 3 * ROWS].astype(BF)
        own[:, where] = value[3 * ROWS :]


def dressed_first(blocks, cyc):
    return pl.pallas_call(
        functools.partial(dressed_kernel, len(cyc)),
        out_shape=[jax.ShapeDtypeStruct((3 * ROWS, QW), BF), jax.ShapeDtypeStruct((ROWS, QW), F32)],
        in_specs=[VMEM] * (4 + len(cyc)),
        out_specs=[VMEM] * 2,
        compiler_params=PARAMS,
        cost_estimate=cost(2 * 512 * PART * 768, 8_000_000),
    )(*blocks, *cyc)


def dressed_last_kernel(*refs):
    blocks, halves, away_in, own_in = refs[:4], refs[4:6], refs[6], refs[7]
    outs, own = refs[8:11], refs[11]
    edge = 3 * 256
    left = jnp.concatenate([blocks[d][...] for d in (1, 2, 3, 0)], 0)
    right = jnp.concatenate([ref[...] for ref in halves], 0)
    value = lax.dot_general(left, right, (((1,), (1,)), ((), ())), preferred_element_type=F32)
    for d in range(3):
        rows = slice(d * ROWS, (d + 1) * ROWS)
        outs[d][:, :edge] = away_in[rows, :edge]
        outs[d][:, edge:] = value[rows].astype(BF)
    own[:, :edge] = own_in[:, :edge]
    own[:, edge:] = value[3 * ROWS :]


def dressed_last(blocks, halves, away, own):
    return pl.pallas_call(
        dressed_last_kernel,
        out_shape=[jax.ShapeDtypeStruct((ROWS, QW), BF)] * 3 + [jax.ShapeDtypeStruct((ROWS, QW), F32)],
        in_specs=[VMEM] * 8,
        out_specs=[VMEM] * 4,
        compiler_params=PARAMS,
        cost_estimate=cost(2 * 512 * PART * 256, 5_000_000),
    )(*blocks, *halves, away, own)


def sum_kernel(own, one, two, three, order, out):
    value = own[...] + one[...].astype(F32) + two[...].astype(F32) + three[...].astype(F32)
    high = value.astype(BF)
    rest = value - high.astype(F32)
    middle = rest.astype(BF)
    low = (rest - middle.astype(F32)).astype(BF)
    moved = jnp.dot(jnp.concatenate([high, middle, low], 0), order[...], preferred_element_type=F32)
    out[...] = moved[:ROWS] + moved[ROWS : 2 * ROWS] + moved[2 * ROWS :]


def group_sum(own, back, order):
    return pl.pallas_call(
        sum_kernel,
        out_shape=jax.ShapeDtypeStruct((ROWS, QW), F32),
        in_specs=[VMEM] * 5,
        out_specs=VMEM,
        compiler_params=PARAMS,
        cost_estimate=cost(6 * ROWS * QW * QW, 4_000_000),
    )(own, *back, order)


def quadratic_kernel(count, *refs):
    lefts, rights, outs = refs[:count], refs[count : count + 9], refs[count + 9 :]
    left = jnp.concatenate([ref[...] for ref in lefts], 0)
    wide = 512
    for n in range(0, PART, wide):
        right = jnp.concatenate([ref[:, n : n + wide] for ref in rights], 0)
        value = jnp.dot(left, right, preferred_element_type=F32).astype(BF)
        for d in range(count):
            outs[d][:, n : n + wide] = value[d * ROWS : (d + 1) * ROWS]


def quadratic_blocks(lefts, rights):
    count = len(lefts)
    return pl.pallas_call(
        functools.partial(quadratic_kernel, count),
        out_shape=[jax.ShapeDtypeStruct((ROWS, PART), BF)] * count,
        in_specs=[VMEM] * (count + 9),
        out_specs=[VMEM] * count,
        compiler_params=PARAMS,
        cost_estimate=cost(2 * count * ROWS * QW * PART, 5_000_000),
    )(*lefts, *rights)


def place_kernel(place, *refs):
    ins, out, sem = refs[:4], refs[4], refs[5]
    copies = []
    for d in range(4):
        at = pl.multiple_of(lax.rem(place[0] + d, 4) * PART, PART)
        for i in range(4):
            rows = slice(i * 32, i * 32 + 32)
            copies.append(
                pltpu.make_async_copy(ins[d].at[rows, :], out.at[rows, pl.ds(at, PART)], sem.at[d * 4 + i])
            )
    for copy in copies:
        copy.start()
    for copy in copies:
        copy.wait()


def place_blocks(place, blocks):
    return pl.pallas_call(
        place_kernel,
        out_shape=jax.ShapeDtypeStruct((ROWS, HALF), BF),
        grid_spec=pltpu.PrefetchScalarGridSpec(
            num_scalar_prefetch=1,
            grid=(),
            in_specs=[VMEM] * 4,
            out_specs=pl.BlockSpec(memory_space=pl.ANY),
            scratch_shapes=[pltpu.SemaphoreType.DMA((16,))],
        ),
        compiler_params=PARAMS,
        cost_estimate=cost(0, 4_000_000),
    )(place, *blocks)


def after(values, *others):
    count = len(values)
    return lax.optimization_barrier(tuple(values) + others)[:count]


def body(amplitudes, cycle_integrals, amp_map, cycle_map):
    row, col, core = (lax.axis_index(a) for a in AX)
    x, y, z = row, col // NZ, col % NZ
    g = jnp.where(core == 0, x, y)
    p = jnp.where(core == 0, y, x)
    place = jnp.stack([g, p, core, row * NY * NZ + col]).astype(jnp.int32)

    shares = small_shares(cycle_map, amp_map, cycle_integrals.T, amplitudes)
    shares = [shares[0]] + [shift_g(shares[4 - d], -d) for d in (1, 2, 3)]
    cyc, win = group_order(place, shares)

    cf, cb = shift_z(cyc, 1), shift_z(cyc, -1)
    window = [win] + [shift_p(win, -e) for e in (1, 2, 3)]
    cf2, cb2 = shift_z(cf, 1), shift_z(cb, -1)
    [amplitudes] = after([amplitudes], cyc)
    mine, *sends = amp_shares(place, amp_map, amplitudes)
    sends = after(sends, cf2, cb2, *window[1:])
    blocks = [mine] + [shift_g(sends[d - 1], d) for d in (1, 2, 3)]
    cf3, cb3 = shift_z(cf2, 1), shift_z(cb2, -1)
    half = cyc.shape[0] // 2
    far = [shift_z(cb3[:half], -1), shift_z(cf3[half:], 1)]
    win = plane_order(place, after(window, *far))
    cyc = stack([cyc, cb, cb2, cb3, *far, cf3, cf2, cf])
    [cyc] = after([cyc], *blocks)

    cf, cb = shift_p(cyc, 1), shift_p(cyc, -1)
    wf, wb = shift_z(win, 1), shift_z(win, -1)
    half = cyc.shape[0] // 2
    far = [shift_p(cb[:half], -1), shift_p(cf[half:], 1)]

    here = lax.broadcasted_iota(jnp.int32, (QW, 1), 0)
    turn, hg = here // 256, here // 8 % 4
    hp = (p + jnp.where(turn == 2, 3, jnp.where(turn == 3, 2, turn))) % 4
    at = jnp.where(core == 0, hg * 32 + hp * 8, hp * 32 + hg * 8)
    there = lax.broadcasted_iota(jnp.int32, (1, QW), 1)
    order = (here // 32 % 8 * 128 + at + here % 8 == there).astype(BF)
    there = lax.broadcasted_iota(jnp.int32, (1, QW // 2), 1) + core * (QW // 2)
    final = (here // 8 % 16 * 64 + (z + here // 128) % NZ * 8 + here % 8 == there).astype(BF)

    away, own = dressed_first(blocks, [cyc, cb, cf])
    wf, wb = after([wf, wb], own)
    wf2, wb2 = shift_z(wf, 1), shift_z(wb, -1)
    *away, own = dressed_last(blocks, far, away, own)
    back = [shift_g(away[d - 1], -d) for d in (1, 2, 3)]
    wf2, wb2 = after([wf2, wb2], back[0])
    wf3, wb3 = shift_z(wf2, 1), shift_z(wb2, -1)
    total = group_sum(own, back, order)
    inner = (total + swap_core(total)).astype(BF)
    inners = [shift_g(inner, d) for d in (1, 2, 3)]
    wf3, wb3 = after([wf3, wb3], inners[0])
    half = win.shape[0] // 2
    far = [shift_z(wb3[:half], -1), shift_z(wf3[half:], 1)]
    rights = [win, wb, wb2, wb3, *far, wf3, wf2, wf]
    dressed = jnp.dot(inner, final, preferred_element_type=F32).astype(BF)

    outs = quadratic_blocks(inners, rights)
    outs = [shift_g(outs[d - 1], -d) for d in (1, 2, 3)]
    outs = list(quadratic_blocks([inner], rights)) + outs
    return (dressed, place_blocks(place, outs))


def solution(mesh):
    placed = (P(("row", "col"), "rep"), P("rep", ("row", "col")), P(("row", "col"), "rep"), P())
    return jax.shard_map(
        body,
        mesh=mesh,
        in_specs=placed,
        out_specs=(P(("row", "col"), "rep"), P(("row", "col"), "rep")),
        check_vma=False,
    )
```

```python
import functools

import jax
import jax.numpy as jnp
from jax import lax
from jax.experimental import pallas as pl
from jax.experimental.pallas import tpu as pltpu
from jax.sharding import PartitionSpec as P

TB = 128
WD = 8
NX, NY, NZ = 4, 4, 8
AX = ("row", "col", "rep")
F32, BF = jnp.float32, jnp.bfloat16
ROWS = 128
HALF = 8192
PART = HALF // 4
QW = 1024
VMEM = pl.BlockSpec(memory_space=pltpu.VMEM)
PARAMS = pltpu.CompilerParams(vmem_limit_bytes=24 * 2**20)


def ident(x, y, z, c):
    return ((x % NX) * NY * NZ + (y % NY) * NZ + z % NZ) * 2 + c


def every():
    return [(x, y, z, c) for x in range(NX) for y in range(NY) for z in range(NZ) for c in (0, 1)]


def shift_z(value, step):
    return lax.ppermute(value, AX, [(ident(x, y, z, c), ident(x, y, z + step, c)) for x, y, z, c in every()])


def shift_plane(value, step, swapped):
    pairs = []
    for x, y, z, c in every():
        if (c == 0) != swapped:
            pairs.append((ident(x, y, z, c), ident(x + step, y, z, c)))
        else:
            pairs.append((ident(x, y, z, c), ident(x, y + step, z, c)))
    return lax.ppermute(value, AX, pairs)


def shift_g(value, step):
    return shift_plane(value, step, False)


def shift_p(value, step):
    return shift_plane(value, step, True)


def swap_core(value):
    return lax.ppermute(value, AX, [(ident(x, y, z, c), ident(x, y, z, 1 - c)) for x, y, z, c in every()])


def cost(flops, moved):
    return pl.CostEstimate(flops=flops, bytes_accessed=moved, transcendentals=0)


def shares_kernel(cyc_map, amp_map, cyc, amp, *refs):
    outs, rows, both, sem = refs[:4], refs[4], refs[5], refs[6]
    row, col, core = (lax.axis_index(a) for a in AX)
    g = jnp.where(core == 0, row, col // NZ)
    copy = pltpu.make_async_copy(amp.at[0:16, :], rows, sem)
    copy.start()
    tiles = HALF // TB
    half_map = cyc_map[pl.ds(pl.multiple_of(core * tiles, tiles), tiles), :].astype(F32)
    lane = lax.broadcasted_iota(jnp.int32, half_map.shape, 1)
    keep = jnp.sum(jnp.where(lane == row * NY * NZ + col, half_map, 0.0), axis=1, keepdims=True)
    keep_window = amp_map[...].astype(F32)
    copy.wait()
    for t in range(tiles):
        at = slice(t * TB, (t + 1) * TB)
        top = cyc[:, at].astype(F32) * keep[t : t + 1, :]
        low = rows[:WD, at].astype(F32) * keep_window[:, t : t + 1]
        both[:, at] = jnp.concatenate([top, low], 0).astype(BF)
    for d in range(4):
        share = pl.multiple_of(lax.rem(g + d, 4) * PART, PART)
        outs[d][...] = both[:, pl.ds(share, PART)]


def small_shares(cycle_map, amp_map, cyc, amplitudes):
    return pl.pallas_call(
        shares_kernel,
        out_shape=[jax.ShapeDtypeStruct((2 * WD, PART), BF)] * 4,
        in_specs=[VMEM] * 3 + [pl.BlockSpec(memory_space=pl.ANY)],
        out_specs=[VMEM] * 4,
        scratch_shapes=[
            pltpu.VMEM((16, HALF), BF),
            pltpu.VMEM((16, HALF), BF),
            pltpu.SemaphoreType.DMA,
        ],
        compiler_params=pltpu.CompilerParams(vmem_limit_bytes=60 * 2**20),
        cost_estimate=cost(0, 600_000),
    )(cycle_map, amp_map, cyc, amplitudes)


def group_kernel(place, *refs):
    pieces, out = refs[:4], refs[4]
    rows = 8 * WD
    here = lax.broadcasted_iota(jnp.int32, (rows, rows), 1)
    there = lax.broadcasted_iota(jnp.int32, (rows, rows), 0)
    member = (here // 16 + place[0]) % 4
    at = member // 2 * 32 + here // 8 % 2 * 16 + member % 2 * 8 + here % 8
    order = (at == there).astype(F32).astype(BF)
    value = jnp.concatenate([ref[...] for ref in pieces], 0)
    out[...] = jnp.dot(order, value, preferred_element_type=F32).astype(BF)


def group_order(place, pieces):
    return pl.pallas_call(
        group_kernel,
        out_shape=jax.ShapeDtypeStruct((8 * WD, PART), BF),
        grid_spec=pltpu.PrefetchScalarGridSpec(
            num_scalar_prefetch=1, grid=(), in_specs=[VMEM] * 4, out_specs=VMEM
        ),
        compiler_params=PARAMS,
        cost_estimate=cost(2 * 64 * 64 * PART, 600_000),
    )(place, *pieces)


def part_kernel(*refs):
    pieces, outs = refs[:9], refs[9:]
    at = 0
    for ref in pieces:
        for rows in range(0, ref.shape[0], 32):
            outs[0][at : at + 16, :] = ref[rows : rows + 16, :]
            outs[1][at : at + 16, :] = ref[rows + 16 : rows + 32, :]
            at += 16


def part(pieces):
    return pl.pallas_call(
        part_kernel,
        out_shape=[jax.ShapeDtypeStruct((32 * WD, PART), BF)] * 2,
        in_specs=[VMEM] * 9,
        out_specs=[VMEM] * 2,
        compiler_params=PARAMS,
        cost_estimate=cost(0, 4_000_000),
    )(*pieces)


def amp_kernel(place, amp_map, *refs):
    ins, outs = refs[:4], refs[4:]
    for d in range(4):
        share = lax.rem(place[0] + d, 4)
        for t in range(PART // TB):
            keep = amp_map[0, share * 16 + t].astype(BF)
            outs[d][:, t * TB : (t + 1) * TB] = ins[d][:, t * TB : (t + 1) * TB] * keep


def amp_shares(place, amp_map, amplitudes):
    block = 32

    def source(d):
        return pl.BlockSpec((block, PART), lambda i, place, amp_map: (i, lax.rem(place[0] + d, 4)))

    return pl.pallas_call(
        amp_kernel,
        out_shape=[jax.ShapeDtypeStruct((ROWS, PART), BF)] * 4,
        grid_spec=pltpu.PrefetchScalarGridSpec(
            num_scalar_prefetch=2,
            grid=(ROWS // block,),
            in_specs=[source(d) for d in range(4)],
            out_specs=[pl.BlockSpec((block, PART), lambda i, place, amp_map: (i, 0))] * 4,
        ),
        compiler_params=PARAMS,
        cost_estimate=cost(0, 4_000_000),
    )(place, amp_map, *[amplitudes] * 4)


def dressed_kernel(count, *refs):
    blocks, cyc = refs[:4], refs[4 : 4 + count]
    away, own = refs[-2:]
    left = jnp.concatenate([blocks[d][...] for d in (1, 2, 3, 0)], 0)
    for at in range(count):
        value = lax.dot_general(left, cyc[at][...], (((1,), (1,)), ((), ())), preferred_element_type=F32)
        where = slice(at * 256, at * 256 + 256)
        away[:, where] = value[: 3 * ROWS].astype(BF)
        own[:, where] = value[3 * ROWS :]


def dressed_first(blocks, cyc):
    return pl.pallas_call(
        functools.partial(dressed_kernel, len(cyc)),
        out_shape=[jax.ShapeDtypeStruct((3 * ROWS, QW), BF), jax.ShapeDtypeStruct((ROWS, QW), F32)],
        in_specs=[VMEM] * (4 + len(cyc)),
        out_specs=[VMEM] * 2,
        compiler_params=PARAMS,
        cost_estimate=cost(2 * 512 * PART * 768, 8_000_000),
    )(*blocks, *cyc)


def dressed_last_kernel(*refs):
    blocks, halves, away_in, own_in = refs[:4], refs[4:6], refs[6], refs[7]
    outs, own = refs[8:11], refs[11]
    edge = 3 * 256
    left = jnp.concatenate([blocks[d][...] for d in (1, 2, 3, 0)], 0)
    right = jnp.concatenate([ref[...] for ref in halves], 0)
    value = lax.dot_general(left, right, (((1,), (1,)), ((), ())), preferred_element_type=F32)
    for d in range(3):
        rows = slice(d * ROWS, (d + 1) * ROWS)
        outs[d][:, :edge] = away_in[rows, :edge]
        outs[d][:, edge:] = value[rows].astype(BF)
    own[:, :edge] = own_in[:, :edge]
    own[:, edge:] = value[3 * ROWS :]


def dressed_last(blocks, halves, away, own):
    return pl.pallas_call(
        dressed_last_kernel,
        out_shape=[jax.ShapeDtypeStruct((ROWS, QW), BF)] * 3 + [jax.ShapeDtypeStruct((ROWS, QW), F32)],
        in_specs=[VMEM] * 8,
        out_specs=[VMEM] * 4,
        compiler_params=PARAMS,
        cost_estimate=cost(2 * 512 * PART * 256, 5_000_000),
    )(*blocks, *halves, away, own)


def inner_kernel(mine, other, order, out):
    value = other[...]
    high = value.astype(BF)
    rest = value - high.astype(F32)
    middle = rest.astype(BF)
    low = (rest - middle.astype(F32)).astype(BF)
    moved = jnp.dot(jnp.concatenate([high, middle, low], 0), order[...], preferred_element_type=F32)
    moved = moved[:ROWS] + moved[ROWS : 2 * ROWS] + moved[2 * ROWS :]
    out[...] = (mine[...] + moved).astype(BF)


def inner_call(mine, other, order):
    return pl.pallas_call(
        inner_kernel,
        out_shape=jax.ShapeDtypeStruct((ROWS, QW), BF),
        in_specs=[VMEM] * 3,
        out_specs=VMEM,
        compiler_params=PARAMS,
        cost_estimate=cost(6 * ROWS * QW * QW, 4_000_000),
    )(mine, other, order)


def quadratic_kernel(count, *refs):
    lefts, rights, outs = refs[:count], refs[count : count + 5], refs[count + 5 :]
    left = jnp.concatenate([ref[...] for ref in lefts], 0)
    wide = 512
    for n in range(0, PART, wide):
        right = jnp.concatenate([ref[:, n : n + wide] for ref in rights], 0)
        value = jnp.dot(left, right, preferred_element_type=F32).astype(BF)
        for d in range(count):
            outs[d][:, n : n + wide] = value[d * ROWS : (d + 1) * ROWS]


def quadratic_blocks(lefts, rights):
    count = len(lefts)
    return pl.pallas_call(
        functools.partial(quadratic_kernel, count),
        out_shape=[jax.ShapeDtypeStruct((ROWS, PART), BF)] * count,
        in_specs=[VMEM] * (count + 5),
        out_specs=[VMEM] * count,
        compiler_params=PARAMS,
        cost_estimate=cost(2 * count * ROWS * QW * PART, 5_000_000),
    )(*lefts, *rights)


def place_kernel(place, *refs):
    ins, out, sem = refs[:4], refs[4], refs[5]
    copies = []
    for d in range(4):
        at = pl.multiple_of(lax.rem(place[0] + d, 4) * PART, PART)
        for i in range(4):
            rows = slice(i * 32, i * 32 + 32)
            copies.append(
                pltpu.make_async_copy(ins[d].at[rows, :], out.at[rows, pl.ds(at, PART)], sem.at[d * 4 + i])
            )
    for copy in copies:
        copy.start()
    for copy in copies:
        copy.wait()


def place_blocks(place, blocks):
    return pl.pallas_call(
        place_kernel,
        out_shape=jax.ShapeDtypeStruct((ROWS, HALF), BF),
        grid_spec=pltpu.PrefetchScalarGridSpec(
            num_scalar_prefetch=1,
            grid=(),
            in_specs=[VMEM] * 4,
            out_specs=pl.BlockSpec(memory_space=pl.ANY),
            scratch_shapes=[pltpu.SemaphoreType.DMA((16,))],
        ),
        compiler_params=PARAMS,
        cost_estimate=cost(0, 4_000_000),
    )(place, *blocks)


def after(values, *others):
    count = len(values)
    return lax.optimization_barrier(tuple(values) + others)[:count]


def body(amplitudes, cycle_integrals, amp_map, cycle_map):
    row, col, core = (lax.axis_index(a) for a in AX)
    x, y, z = row, col // NZ, col % NZ
    g = jnp.where(core == 0, x, y)
    p = jnp.where(core == 0, y, x)
    place = jnp.stack([g, p, core, row * NY * NZ + col]).astype(jnp.int32)

    shares = small_shares(cycle_map, amp_map, cycle_integrals.T, amplitudes)
    [amplitudes] = after([amplitudes], shares[0])
    shares = [shares[0]] + [shift_g(shares[4 - d], -d) for d in (1, 2, 3)]
    mine, *sends = amp_shares(place, amp_map, amplitudes)
    both = group_order(place, after(shares, mine))

    f, b = shift_z(both, 1), shift_z(both, -1)
    f2, b2 = shift_z(f, 1), shift_z(b, -1)
    sends[:2] = after(sends[:2], f)
    f3, b3 = shift_z(f2, 1), shift_z(b2, -1)
    sends[2:] = after(sends[2:], f2)
    half = both.shape[0] // 2
    far = [shift_z(b3[:half], -1), shift_z(f3[half:], 1)]
    blocks = [mine] + [shift_g(sends[d - 1], d) for d in (1, 2, 3)]
    cyc, win = part([both, b, b2, b3, *far, f3, f2, f])
    [cyc] = after([cyc], *blocks)

    cf, cb = shift_p(cyc, 1), shift_p(cyc, -1)
    half = cyc.shape[0] // 2
    far = [shift_p(cb[:half], -1), shift_p(cf[half:], 1)]

    here = lax.broadcasted_iota(jnp.int32, (QW, 1), 0)
    turn, spot, hg, hw = here // 256, here // 32 % 8, here // 8 % 4, here % 8
    turn = jnp.where(turn == 2, 3, jnp.where(turn == 3, 2, turn))
    turn_here = (hg - p) % 4
    turn_here = jnp.where(turn_here == 2, 3, jnp.where(turn_here == 3, 2, turn_here))
    there = lax.broadcasted_iota(jnp.int32, (1, QW), 1)
    order = (turn_here * 256 + spot * 32 + (g + turn) % 4 * 8 + hw == there).astype(BF)
    hp = (p + turn) % 4
    hx, hy = jnp.where(core == 0, hg, hp), jnp.where(core == 0, hp, hg)
    there = lax.broadcasted_iota(jnp.int32, (1, QW // 2), 1) + core * (QW // 2)
    final = (hx * 256 + hy * 64 + (z + spot) % NZ * 8 + hw == there).astype(BF)

    away, own = dressed_first(blocks, [cyc, cb, cf])
    [win] = after([win], own)
    wf, wb = shift_p(win, 1), shift_p(win, -1)
    *away, total = dressed_last(blocks, far, away, own)
    back = [shift_g(away[d - 1], -d) for d in (1, 2, 3)]
    for value in back:
        total = total + value.astype(F32)
    inner = inner_call(total, swap_core(total), order)
    inners = [shift_g(inner, d) for d in (1, 2, 3)]
    rights = [win, wb, wf, shift_p(wb[:half], -1), shift_p(wf[half:], 1)]
    dressed = jnp.dot(inner, final, preferred_element_type=F32).astype(BF)

    outs = quadratic_blocks(inners, rights)
    outs = [shift_g(outs[d - 1], -d) for d in (1, 2, 3)]
    outs = list(quadratic_blocks([inner], rights)) + outs
    return (dressed, place_blocks(place, outs))


def solution(mesh):
    placed = (P(("row", "col"), "rep"), P("rep", ("row", "col")), P(("row", "col"), "rep"), P())
    return jax.shard_map(
        body,
        mesh=mesh,
        in_specs=placed,
        out_specs=(P(("row", "col"), "rep"), P(("row", "col"), "rep")),
        check_vma=False,
    )
```

```python
import functools

import jax
import jax.numpy as jnp
from jax import lax
from jax.experimental import pallas as pl
from jax.experimental.pallas import tpu as pltpu
from jax.sharding import PartitionSpec as P

TB = 128
WD = 8
NX, NY, NZ = 4, 4, 8
AX = ("row", "col", "rep")
F32, BF = jnp.float32, jnp.bfloat16
ROWS = 128
HALF = 8192
PART = HALF // 4
QW = 1024
EARLY = 5 * 32
LATE = 3 * 32
VMEM = pl.BlockSpec(memory_space=pltpu.VMEM)
PARAMS = pltpu.CompilerParams(vmem_limit_bytes=8 * 2**20)
WIDE = pltpu.CompilerParams(vmem_limit_bytes=16 * 2**20)


def ident(x, y, z, c):
    return ((x % NX) * NY * NZ + (y % NY) * NZ + z % NZ) * 2 + c


def every():
    return [(x, y, z, c) for x in range(NX) for y in range(NY) for z in range(NZ) for c in (0, 1)]


def shift_z(value, step):
    return lax.ppermute(value, AX, [(ident(x, y, z, c), ident(x, y, z + step, c)) for x, y, z, c in every()])


def shift_plane(value, step, swapped):
    pairs = []
    for x, y, z, c in every():
        if (c == 0) != swapped:
            pairs.append((ident(x, y, z, c), ident(x + step, y, z, c)))
        else:
            pairs.append((ident(x, y, z, c), ident(x, y + step, z, c)))
    return lax.ppermute(value, AX, pairs)


def shift_g(value, step):
    return shift_plane(value, step, False)


def shift_p(value, step):
    return shift_plane(value, step, True)


def swap_core(value):
    return lax.ppermute(value, AX, [(ident(x, y, z, c), ident(x, y, z, 1 - c)) for x, y, z, c in every()])


def cost(flops, moved):
    return pl.CostEstimate(flops=flops, bytes_accessed=moved, transcendentals=0)


def shares_kernel(cyc_map_in, amp_map_in, cyc_in, amp, *refs):
    outs, rows, both, half_map, amp_map, cyc, sem = refs[:4], *refs[4:]
    row, col, core = (lax.axis_index(a) for a in AX)
    g = jnp.where(core == 0, row, col // NZ)
    tiles = HALF // TB
    mine = cyc_map_in.at[pl.ds(pl.multiple_of(core * tiles, tiles), tiles), :]
    pairs = [(mine, half_map), (amp_map_in, amp_map), (cyc_in, cyc), (amp.at[0:16, :], rows)]
    copies = [pltpu.make_async_copy(pairs[i][0], pairs[i][1], sem.at[i]) for i in range(4)]
    for copy in copies:
        copy.start()
    for copy in copies:
        copy.wait()
    half_map = half_map[...].astype(F32)
    lane = lax.broadcasted_iota(jnp.int32, half_map.shape, 1)
    keep = jnp.sum(jnp.where(lane == row * NY * NZ + col, half_map, 0.0), axis=1, keepdims=True)
    keep_window = amp_map[...].astype(F32)
    for t in range(tiles):
        at = slice(t * TB, (t + 1) * TB)
        top = cyc[:, at].astype(F32) * keep[t : t + 1, :]
        low = rows[:WD, at].astype(F32) * keep_window[:, t : t + 1]
        both[:, at] = jnp.concatenate([top, low], 0).astype(BF)
    for d in range(4):
        share = pl.multiple_of(lax.rem(g + d, 4) * PART, PART)
        outs[d][...] = both[:, pl.ds(share, PART)]


def small_shares(cycle_map, amp_map, cyc, amplitudes):
    return pl.pallas_call(
        shares_kernel,
        out_shape=[jax.ShapeDtypeStruct((2 * WD, PART), BF)] * 4,
        in_specs=[pl.BlockSpec(memory_space=pl.ANY)] * 4,
        out_specs=[VMEM] * 4,
        scratch_shapes=[
            pltpu.VMEM((16, HALF), BF),
            pltpu.VMEM((16, HALF), BF),
            pltpu.VMEM((HALF // TB, 128), jnp.int32),
            pltpu.VMEM((1, HALF // TB), jnp.int32),
            pltpu.VMEM((WD, HALF), BF),
            pltpu.SemaphoreType.DMA((4,)),
        ],
        compiler_params=pltpu.CompilerParams(vmem_limit_bytes=60 * 2**20),
        cost_estimate=cost(0, 600_000),
    )(cycle_map, amp_map, cyc, amplitudes)


def group_kernel(place, *refs):
    pieces, out = refs[:4], refs[4]
    rows = 8 * WD
    here = lax.broadcasted_iota(jnp.int32, (rows, rows), 1)
    there = lax.broadcasted_iota(jnp.int32, (rows, rows), 0)
    member = (here // 16 + place[0]) % 4
    at = member // 2 * 32 + here // 8 % 2 * 16 + member % 2 * 8 + here % 8
    order = (at == there).astype(F32).astype(BF)
    value = jnp.concatenate([ref[...] for ref in pieces], 0)
    out[...] = jnp.dot(order, value, preferred_element_type=F32).astype(BF)


def group_order(place, pieces):
    return pl.pallas_call(
        group_kernel,
        out_shape=jax.ShapeDtypeStruct((8 * WD, PART), BF),
        grid_spec=pltpu.PrefetchScalarGridSpec(
            num_scalar_prefetch=1, grid=(), in_specs=[VMEM] * 4, out_specs=VMEM
        ),
        compiler_params=PARAMS,
        cost_estimate=cost(2 * 64 * 64 * PART, 600_000),
    )(place, *pieces)


def late_kernel(*refs):
    outs = refs[9:]
    at = 0
    for ref in refs[:9]:
        for rows in range(0, ref.shape[0], 32):
            if at >= EARLY:
                outs[0][at - EARLY : at - EARLY + 16, :] = ref[rows : rows + 16, :]
            outs[1][at : at + 16, :] = ref[rows + 16 : rows + 32, :]
            at += 16


def early_kernel(*refs):
    at = 0
    for ref in refs[:5]:
        for rows in range(0, ref.shape[0], 32):
            refs[5][at : at + 16, :] = ref[rows : rows + 16, :]
            at += 16


def part_early(pieces):
    return pl.pallas_call(
        early_kernel,
        out_shape=jax.ShapeDtypeStruct((EARLY, PART), BF),
        in_specs=[VMEM] * 5,
        out_specs=VMEM,
        compiler_params=PARAMS,
        cost_estimate=cost(0, 1_300_000),
    )(*pieces)


def part_late(pieces):
    return pl.pallas_call(
        late_kernel,
        out_shape=[
            jax.ShapeDtypeStruct((LATE, PART), BF),
            jax.ShapeDtypeStruct((EARLY + LATE, PART), BF),
        ],
        in_specs=[VMEM] * 9,
        out_specs=[VMEM] * 2,
        compiler_params=PARAMS,
        cost_estimate=cost(0, 4_000_000),
    )(*pieces)


def amp_kernel(place, amp_map, *refs):
    ins, outs = refs[:4], refs[4:]
    for d in range(4):
        share = lax.rem(place[0] + d, 4)
        for t in range(PART // TB):
            keep = amp_map[0, share * 16 + t].astype(BF)
            outs[d][:, t * TB : (t + 1) * TB] = ins[d][:, t * TB : (t + 1) * TB] * keep


def amp_shares(place, amp_map, amplitudes):
    block = 32

    def source(d):
        return pl.BlockSpec((block, PART), lambda i, place, amp_map: (i, lax.rem(place[0] + d, 4)))

    return pl.pallas_call(
        amp_kernel,
        out_shape=[jax.ShapeDtypeStruct((ROWS, PART), BF)] * 4,
        grid_spec=pltpu.PrefetchScalarGridSpec(
            num_scalar_prefetch=2,
            grid=(ROWS // block,),
            in_specs=[source(d) for d in range(4)],
            out_specs=[pl.BlockSpec((block, PART), lambda i, place, amp_map: (i, 0))] * 4,
        ),
        compiler_params=PARAMS,
        cost_estimate=cost(0, 4_000_000),
    )(place, amp_map, *[amplitudes] * 4)


def product(blocks, cyc):
    left = jnp.concatenate([blocks[d][...] for d in (1, 2, 3, 0)], 0)
    right = jnp.concatenate([ref[...] for ref in cyc], 0)
    return lax.dot_general(left, right, (((1,), (1,)), ((), ())), preferred_element_type=F32)


def dressed_first_kernel(*refs):
    value = product(refs[:4], refs[4:9])
    refs[9][...] = value[: 3 * ROWS].astype(BF)
    refs[10][...] = value[3 * ROWS :]


def dressed_first(blocks, cyc):
    return pl.pallas_call(
        dressed_first_kernel,
        out_shape=[
            jax.ShapeDtypeStruct((3 * ROWS, 4 * EARLY), BF),
            jax.ShapeDtypeStruct((ROWS, 4 * EARLY), F32),
        ],
        in_specs=[VMEM] * 9,
        out_specs=[VMEM] * 2,
        compiler_params=WIDE,
        cost_estimate=cost(2 * 512 * PART * 4 * EARLY, 6_000_000),
    )(*blocks, *cyc)


def dressed_last_kernel(*refs):
    away, early, outs, own = refs[9], refs[10], refs[11:14], refs[14]
    edge = 4 * EARLY
    value = product(refs[:4], refs[4:9])
    for d in range(3):
        rows = slice(d * ROWS, (d + 1) * ROWS)
        outs[d][:, :edge] = away[rows, :]
        outs[d][:, edge:] = value[rows].astype(BF)
    own[:, :edge] = early[...]
    own[:, edge:] = value[3 * ROWS :]


def dressed_last(blocks, cyc, away, early):
    return pl.pallas_call(
        dressed_last_kernel,
        out_shape=[jax.ShapeDtypeStruct((ROWS, QW), BF)] * 3 + [jax.ShapeDtypeStruct((ROWS, QW), F32)],
        in_specs=[VMEM] * 11,
        out_specs=[VMEM] * 4,
        compiler_params=WIDE,
        cost_estimate=cost(2 * 512 * PART * 4 * LATE, 6_000_000),
    )(*blocks, *cyc, away, early)


def inner_kernel(mine, other, order, out):
    value = other[...]
    high = value.astype(BF)
    rest = value - high.astype(F32)
    middle = rest.astype(BF)
    low = (rest - middle.astype(F32)).astype(BF)
    moved = jnp.dot(jnp.concatenate([high, middle, low], 0), order[...], preferred_element_type=F32)
    moved = moved[:ROWS] + moved[ROWS : 2 * ROWS] + moved[2 * ROWS :]
    out[...] = (mine[...] + moved).astype(BF)


def inner_call(mine, other, order):
    return pl.pallas_call(
        inner_kernel,
        out_shape=jax.ShapeDtypeStruct((ROWS, QW), BF),
        in_specs=[VMEM] * 3,
        out_specs=VMEM,
        compiler_params=PARAMS,
        cost_estimate=cost(6 * ROWS * QW * QW, 4_000_000),
    )(mine, other, order)


def quadratic_kernel(count, *refs):
    lefts, rights, outs = refs[:count], refs[count : count + 5], refs[count + 5 :]
    left = jnp.concatenate([ref[...] for ref in lefts], 0)
    mine, above, half, other, below = rights
    middle = half.shape[0]
    wide = 512
    for n in range(0, PART, wide):
        cols = slice(n, n + wide)
        right = [mine[:EARLY, cols], above[:EARLY, cols], half[:, cols], other[: EARLY - middle, cols]]
        right += [below[:EARLY, cols], mine[EARLY:, cols], above[EARLY:, cols]]
        right += [other[EARLY - middle :, cols], below[EARLY:, cols]]
        value = jnp.dot(left, jnp.concatenate(right, 0), preferred_element_type=F32).astype(BF)
        for d in range(count):
            outs[d][:, cols] = value[d * ROWS : (d + 1) * ROWS]


def quadratic_blocks(lefts, rights):
    count = len(lefts)
    return pl.pallas_call(
        functools.partial(quadratic_kernel, count),
        out_shape=[jax.ShapeDtypeStruct((ROWS, PART), BF)] * count,
        in_specs=[VMEM] * (count + 5),
        out_specs=[VMEM] * count,
        compiler_params=WIDE,
        cost_estimate=cost(2 * count * ROWS * QW * PART, 5_000_000),
    )(*lefts, *rights)


def place_kernel(ds, place, *refs):
    ins, out, sem = refs[: len(ds)], refs[-2], refs[-1]
    copies = []
    for k, d in enumerate(ds):
        at = pl.multiple_of(lax.rem(place[0] + d, 4) * PART, PART)
        for i in range(4):
            rows = slice(i * 32, i * 32 + 32)
            copies.append(
                pltpu.make_async_copy(ins[k].at[rows, :], out.at[rows, pl.ds(at, PART)], sem.at[k * 4 + i])
            )
    for copy in copies:
        copy.start()
    for copy in copies:
        copy.wait()


def place_blocks(place, blocks, out=None):
    anywhere = pl.BlockSpec(memory_space=pl.ANY)
    ds = tuple(blocks)
    operands = [place] + [blocks[d] for d in ds] + ([] if out is None else [out])
    return pl.pallas_call(
        functools.partial(place_kernel, ds),
        out_shape=jax.ShapeDtypeStruct((ROWS, HALF), BF),
        grid_spec=pltpu.PrefetchScalarGridSpec(
            num_scalar_prefetch=1,
            grid=(),
            in_specs=[VMEM] * len(ds) + ([] if out is None else [anywhere]),
            out_specs=anywhere,
            scratch_shapes=[pltpu.SemaphoreType.DMA((4 * len(ds),))],
        ),
        input_output_aliases={} if out is None else {len(operands) - 1: 0},
        compiler_params=PARAMS,
        cost_estimate=cost(0, 1_000_000 * len(ds)),
    )(*operands)


def after(values, *others):
    count = len(values)
    return lax.optimization_barrier(tuple(values) + others)[:count]


def body(amplitudes, cycle_integrals, amp_map, cycle_map):
    row, col, core = (lax.axis_index(a) for a in AX)
    x, y, z = row, col // NZ, col % NZ
    g = jnp.where(core == 0, x, y)
    p = jnp.where(core == 0, y, x)
    place = jnp.stack([g, p, core, row * NY * NZ + col]).astype(jnp.int32)

    shares = small_shares(cycle_map, amp_map, cycle_integrals.T, amplitudes)
    [amplitudes] = after([amplitudes], shares[0])
    shares = [shares[0]] + [shift_g(shares[4 - d], -d) for d in (1, 2, 3)]
    mine, *sends = amp_shares(place, amp_map, amplitudes)
    both = group_order(place, after(shares, mine))

    f, b = shift_z(both, 1), shift_z(both, -1)
    sends = after(sends, both)
    blocks = [mine] + [shift_g(sends[d - 1], d) for d in (1, 2, 3)]
    f2, b2 = shift_z(f, 1), shift_z(b, -1)
    pieces = [both, b, f, b2, f2]
    early = part_early(after(pieces, *blocks[1:]))
    f3, b3 = shift_z(f2, 1), shift_z(b2, -1)
    ef, eb = shift_p(early, 1), shift_p(early, -1)
    half = both.shape[0] // 2
    pieces += [b3, f3, shift_z(b3[:half], -1), shift_z(f3[half:], 1)]
    late, win = part_late(pieces)
    lf, lb = shift_p(late, 1), shift_p(late, -1)
    half = EARLY // 2
    early = [early, eb, shift_p(eb[:half], -1), shift_p(ef[half:], 1), ef]
    half = LATE // 2
    late = [late, lb, shift_p(lb[:half], -1), shift_p(lf[half:], 1), lf]

    here = lax.broadcasted_iota(jnp.int32, (QW, 1), 0)
    rest = here - 4 * EARLY
    soon = rest < 0
    turn = jnp.where(soon, here // EARLY, rest // LATE)
    spot = jnp.where(soon, here % EARLY // 32, EARLY // 32 + rest % LATE // 32)
    hg, hw = here // 8 % 4, here % 8
    turn_here = (hg - p) % 4
    at = jnp.where(soon, turn_here * EARLY, 4 * EARLY + turn_here * LATE - EARLY) + spot * 32
    there = lax.broadcasted_iota(jnp.int32, (1, QW), 1)
    order = (at + (g + turn) % 4 * 8 + hw == there).astype(BF)
    hp = (p + turn) % 4
    hx, hy = jnp.where(core == 0, hg, hp), jnp.where(core == 0, hp, hg)
    hz = (z + jnp.where(spot % 2 == 1, (spot + 1) // 2, 8 - spot // 2)) % NZ
    there = lax.broadcasted_iota(jnp.int32, (1, QW // 2), 1) + core * (QW // 2)
    final = (hx * 256 + hy * 64 + hz * 8 + hw == there).astype(BF)

    away, own = dressed_first(blocks, early)
    [win] = after([win], late[2])
    wf, wb = shift_p(win, 1), shift_p(win, -1)
    *away, total = dressed_last(blocks, late, away, own)
    back = [shift_g(away[d - 1], -d) for d in (1, 2, 3)]
    for value in back:
        total = total + value.astype(F32)
    inner = inner_call(total, swap_core(total), order)
    inners = [shift_g(inner, d) for d in (1, 2, 3)]
    half = win.shape[0] // 2
    rights = [win, wb, shift_p(wb[:half], -1), shift_p(wf[half:], 1), wf]
    dressed = jnp.dot(inner, final, preferred_element_type=F32).astype(BF)

    outs = {}
    for d in (2, 1, 3):
        [value] = quadratic_blocks([inners[d - 1]], rights)
        outs[d] = shift_g(value, -d)
    [outs[0]] = quadratic_blocks([inner], rights)
    quadratic = place_blocks(place, {d: outs[d] for d in (0, 1, 2)})
    quadratic = place_blocks(place, {3: outs[3]}, quadratic)
    return (dressed, quadratic)


def solution(mesh):
    placed = (P(("row", "col"), "rep"), P("rep", ("row", "col")), P(("row", "col"), "rep"), P())
    return jax.shard_map(
        body,
        mesh=mesh,
        in_specs=placed,
        out_specs=(P(("row", "col"), "rep"), P(("row", "col"), "rep")),
        check_vma=False,
    )
```

```python
import functools

import jax
import jax.numpy as jnp
from jax import lax
from jax.experimental import pallas as pl
from jax.experimental.pallas import tpu as pltpu
from jax.sharding import PartitionSpec as P

TB = 128
WD = 8
NX, NY, NZ = 4, 4, 8
AX = ("row", "col", "rep")
F32, BF = jnp.float32, jnp.bfloat16
ROWS = 128
HALF = 8192
PART = HALF // 4
QW = 1024
EARLY = 5 * 32
LATE = 3 * 32
VMEM = pl.BlockSpec(memory_space=pltpu.VMEM)
PARAMS = pltpu.CompilerParams(vmem_limit_bytes=8 * 2**20)
WIDE = pltpu.CompilerParams(vmem_limit_bytes=16 * 2**20)


def ident(x, y, z, c):
    return ((x % NX) * NY * NZ + (y % NY) * NZ + z % NZ) * 2 + c


def every():
    return [(x, y, z, c) for x in range(NX) for y in range(NY) for z in range(NZ) for c in (0, 1)]


def shift_z(value, step):
    return lax.ppermute(value, AX, [(ident(x, y, z, c), ident(x, y, z + step, c)) for x, y, z, c in every()])


def shift_plane(value, step, swapped):
    pairs = []
    for x, y, z, c in every():
        if (c == 0) != swapped:
            pairs.append((ident(x, y, z, c), ident(x + step, y, z, c)))
        else:
            pairs.append((ident(x, y, z, c), ident(x, y + step, z, c)))
    return lax.ppermute(value, AX, pairs)


def shift_g(value, step):
    return shift_plane(value, step, False)


def shift_p(value, step):
    return shift_plane(value, step, True)


def swap_core(value):
    return lax.ppermute(value, AX, [(ident(x, y, z, c), ident(x, y, z, 1 - c)) for x, y, z, c in every()])


def cost(flops, moved):
    return pl.CostEstimate(flops=flops, bytes_accessed=moved, transcendentals=0)


def shares_kernel(cyc_map_in, amp_map_in, cyc_in, amp, *refs):
    outs, rows, both, half_map, amp_map, cyc, sem = refs[:4], *refs[4:]
    row, col, core = (lax.axis_index(a) for a in AX)
    g = jnp.where(core == 0, row, col // NZ)
    tiles = HALF // TB
    mine = cyc_map_in.at[pl.ds(pl.multiple_of(core * tiles, tiles), tiles), :]
    pairs = [(mine, half_map), (amp_map_in, amp_map), (cyc_in, cyc), (amp.at[0:16, :], rows)]
    copies = [pltpu.make_async_copy(pairs[i][0], pairs[i][1], sem.at[i]) for i in range(4)]
    for copy in copies:
        copy.start()
    for copy in copies:
        copy.wait()
    half_map = half_map[...].astype(F32)
    lane = lax.broadcasted_iota(jnp.int32, half_map.shape, 1)
    keep = jnp.sum(jnp.where(lane == row * NY * NZ + col, half_map, 0.0), axis=1, keepdims=True)
    keep_window = amp_map[...].astype(F32)
    for t in range(tiles):
        at = slice(t * TB, (t + 1) * TB)
        top = cyc[:, at].astype(F32) * keep[t : t + 1, :]
        low = rows[:WD, at].astype(F32) * keep_window[:, t : t + 1]
        both[:, at] = jnp.concatenate([top, low], 0).astype(BF)
    for d in range(4):
        share = pl.multiple_of(lax.rem(g + d, 4) * PART, PART)
        outs[d][...] = both[:, pl.ds(share, PART)]


def small_shares(cycle_map, amp_map, cyc, amplitudes):
    return pl.pallas_call(
        shares_kernel,
        out_shape=[jax.ShapeDtypeStruct((2 * WD, PART), BF)] * 4,
        in_specs=[pl.BlockSpec(memory_space=pl.ANY)] * 4,
        out_specs=[VMEM] * 4,
        scratch_shapes=[
            pltpu.VMEM((16, HALF), BF),
            pltpu.VMEM((16, HALF), BF),
            pltpu.VMEM((HALF // TB, 128), jnp.int32),
            pltpu.VMEM((1, HALF // TB), jnp.int32),
            pltpu.VMEM((WD, HALF), BF),
            pltpu.SemaphoreType.DMA((4,)),
        ],
        compiler_params=pltpu.CompilerParams(vmem_limit_bytes=60 * 2**20),
        cost_estimate=cost(0, 600_000),
    )(cycle_map, amp_map, cyc, amplitudes)


def group_kernel(place, *refs):
    pieces, out = refs[:4], refs[4]
    rows = 8 * WD
    here = lax.broadcasted_iota(jnp.int32, (rows, rows), 1)
    there = lax.broadcasted_iota(jnp.int32, (rows, rows), 0)
    member = (here // 16 + place[0]) % 4
    at = member // 2 * 32 + here // 8 % 2 * 16 + member % 2 * 8 + here % 8
    order = (at == there).astype(F32).astype(BF)
    value = jnp.concatenate([ref[...] for ref in pieces], 0)
    out[...] = jnp.dot(order, value, preferred_element_type=F32).astype(BF)


def group_order(place, pieces):
    return pl.pallas_call(
        group_kernel,
        out_shape=jax.ShapeDtypeStruct((8 * WD, PART), BF),
        grid_spec=pltpu.PrefetchScalarGridSpec(
            num_scalar_prefetch=1, grid=(), in_specs=[VMEM] * 4, out_specs=VMEM
        ),
        compiler_params=PARAMS,
        cost_estimate=cost(2 * 64 * 64 * PART, 600_000),
    )(place, *pieces)


def late_kernel(*refs):
    outs = refs[9:]
    at = 0
    for ref in refs[:9]:
        for rows in range(0, ref.shape[0], 32):
            if at >= EARLY:
                outs[0][at - EARLY : at - EARLY + 16, :] = ref[rows : rows + 16, :]
            outs[1][at : at + 16, :] = ref[rows + 16 : rows + 32, :]
            at += 16


def early_kernel(*refs):
    at = 0
    for ref in refs[:5]:
        for rows in range(0, ref.shape[0], 32):
            refs[5][at : at + 16, :] = ref[rows : rows + 16, :]
            at += 16


def part_early(pieces):
    return pl.pallas_call(
        early_kernel,
        out_shape=jax.ShapeDtypeStruct((EARLY, PART), BF),
        in_specs=[VMEM] * 5,
        out_specs=VMEM,
        compiler_params=PARAMS,
        cost_estimate=cost(0, 1_300_000),
    )(*pieces)


def part_late(pieces):
    return pl.pallas_call(
        late_kernel,
        out_shape=[
            jax.ShapeDtypeStruct((LATE, PART), BF),
            jax.ShapeDtypeStruct((EARLY + LATE, PART), BF),
        ],
        in_specs=[VMEM] * 9,
        out_specs=[VMEM] * 2,
        compiler_params=PARAMS,
        cost_estimate=cost(0, 4_000_000),
    )(*pieces)


def amp_kernel(place, amp_map, *refs):
    ins, outs = refs[:4], refs[4:]
    for d in range(4):
        share = lax.rem(place[0] + d, 4)
        for t in range(PART // TB):
            keep = amp_map[0, share * 16 + t].astype(BF)
            outs[d][:, t * TB : (t + 1) * TB] = ins[d][:, t * TB : (t + 1) * TB] * keep


def amp_shares(place, amp_map, amplitudes):
    block = 32

    def source(d):
        return pl.BlockSpec((block, PART), lambda i, place, amp_map: (i, lax.rem(place[0] + d, 4)))

    return pl.pallas_call(
        amp_kernel,
        out_shape=[jax.ShapeDtypeStruct((ROWS, PART), BF)] * 4,
        grid_spec=pltpu.PrefetchScalarGridSpec(
            num_scalar_prefetch=2,
            grid=(ROWS // block,),
            in_specs=[source(d) for d in range(4)],
            out_specs=[pl.BlockSpec((block, PART), lambda i, place, amp_map: (i, 0))] * 4,
        ),
        compiler_params=PARAMS,
        cost_estimate=cost(0, 4_000_000),
    )(place, amp_map, *[amplitudes] * 4)


def product(blocks, cyc):
    left = jnp.concatenate([blocks[d][...] for d in (1, 2, 3, 0)], 0)
    right = jnp.concatenate([ref[...] for ref in cyc], 0)
    return lax.dot_general(left, right, (((1,), (1,)), ((), ())), preferred_element_type=F32)


def dressed_first_kernel(*refs):
    value = product(refs[:4], refs[4:9])
    refs[9][...] = value[: 3 * ROWS].astype(BF)
    refs[10][...] = value[3 * ROWS :]


def dressed_first(blocks, cyc):
    return pl.pallas_call(
        dressed_first_kernel,
        out_shape=[
            jax.ShapeDtypeStruct((3 * ROWS, 4 * EARLY), BF),
            jax.ShapeDtypeStruct((ROWS, 4 * EARLY), F32),
        ],
        in_specs=[VMEM] * 9,
        out_specs=[VMEM] * 2,
        compiler_params=WIDE,
        cost_estimate=cost(2 * 512 * PART * 4 * EARLY, 6_000_000),
    )(*blocks, *cyc)


def dressed_last_kernel(*refs):
    away, early, outs, own = refs[9], refs[10], refs[11:14], refs[14]
    edge = 4 * EARLY
    value = product(refs[:4], refs[4:9])
    for d in range(3):
        rows = slice(d * ROWS, (d + 1) * ROWS)
        outs[d][:, :edge] = away[rows, :]
        outs[d][:, edge:] = value[rows].astype(BF)
    own[:, :edge] = early[...]
    own[:, edge:] = value[3 * ROWS :]


def dressed_last(blocks, cyc, away, early):
    return pl.pallas_call(
        dressed_last_kernel,
        out_shape=[jax.ShapeDtypeStruct((ROWS, QW), BF)] * 3 + [jax.ShapeDtypeStruct((ROWS, QW), F32)],
        in_specs=[VMEM] * 11,
        out_specs=[VMEM] * 4,
        compiler_params=WIDE,
        cost_estimate=cost(2 * 512 * PART * 4 * LATE, 6_000_000),
    )(*blocks, *cyc, away, early)


def inner_kernel(mine, other, order, out):
    value = other[...]
    high = value.astype(BF)
    rest = value - high.astype(F32)
    middle = rest.astype(BF)
    low = (rest - middle.astype(F32)).astype(BF)
    moved = jnp.dot(jnp.concatenate([high, middle, low], 0), order[...], preferred_element_type=F32)
    moved = moved[:ROWS] + moved[ROWS : 2 * ROWS] + moved[2 * ROWS :]
    out[...] = (mine[...] + moved).astype(BF)


def inner_call(mine, other, order):
    return pl.pallas_call(
        inner_kernel,
        out_shape=jax.ShapeDtypeStruct((ROWS, QW), BF),
        in_specs=[VMEM] * 3,
        out_specs=VMEM,
        compiler_params=PARAMS,
        cost_estimate=cost(6 * ROWS * QW * QW, 4_000_000),
    )(mine, other, order)


def quadratic_kernel(count, *refs):
    lefts, rights, outs = refs[:count], refs[count : count + 5], refs[count + 5 :]
    left = jnp.concatenate([ref[...] for ref in lefts], 0)
    mine, above, half, other, below = rights
    middle = half.shape[0]
    wide = 512
    for n in range(0, PART, wide):
        cols = slice(n, n + wide)
        right = [mine[:EARLY, cols], above[:EARLY, cols], half[:, cols], other[: EARLY - middle, cols]]
        right += [below[:EARLY, cols], mine[EARLY:, cols], above[EARLY:, cols]]
        right += [other[EARLY - middle :, cols], below[EARLY:, cols]]
        value = jnp.dot(left, jnp.concatenate(right, 0), preferred_element_type=F32).astype(BF)
        for d in range(count):
            outs[d][:, cols] = value[d * ROWS : (d + 1) * ROWS]


def quadratic_blocks(lefts, rights):
    count = len(lefts)
    return pl.pallas_call(
        functools.partial(quadratic_kernel, count),
        out_shape=[jax.ShapeDtypeStruct((ROWS, PART), BF)] * count,
        in_specs=[VMEM] * (count + 5),
        out_specs=[VMEM] * count,
        compiler_params=WIDE,
        cost_estimate=cost(2 * count * ROWS * QW * PART, 5_000_000),
    )(*lefts, *rights)


def place_kernel(ds, place, *refs):
    ins, out, held, sem = refs[: len(ds)], refs[-3], refs[-2], refs[-1]
    chunks = [(k, slice(i * 32, i * 32 + 32)) for k in range(len(ds)) for i in range(4)]
    copies = []
    for n, (k, rows) in enumerate(chunks):
        copies.append(pltpu.make_async_copy(ins[k].at[rows, :], held.at[k, rows, :], sem.at[n]))
    for copy in copies:
        copy.start()
    later = []
    for n, (k, rows) in enumerate(chunks):
        at = pl.multiple_of(lax.rem(place[0] + ds[k], 4) * PART, PART)
        copies[n].wait()
        to = out.at[rows, pl.ds(at, PART)]
        later.append(pltpu.make_async_copy(held.at[k, rows, :], to, sem.at[len(chunks) + n]))
        later[-1].start()
    for copy in later:
        copy.wait()


def place_blocks(place, blocks, out=None):
    anywhere = pl.BlockSpec(memory_space=pl.ANY)
    ds = tuple(blocks)
    operands = [place] + [blocks[d] for d in ds] + ([] if out is None else [out])
    return pl.pallas_call(
        functools.partial(place_kernel, ds),
        out_shape=jax.ShapeDtypeStruct((ROWS, HALF), BF),
        grid_spec=pltpu.PrefetchScalarGridSpec(
            num_scalar_prefetch=1,
            grid=(),
            in_specs=[anywhere] * (len(operands) - 1),
            out_specs=anywhere,
            scratch_shapes=[
                pltpu.VMEM((len(ds), ROWS, PART), BF),
                pltpu.SemaphoreType.DMA((8 * len(ds),)),
            ],
        ),
        input_output_aliases={} if out is None else {len(operands) - 1: 0},
        compiler_params=PARAMS,
        cost_estimate=cost(0, 1_000_000 * len(ds)),
    )(*operands)


def after(values, *others):
    count = len(values)
    return lax.optimization_barrier(tuple(values) + others)[:count]


def body(amplitudes, cycle_integrals, amp_map, cycle_map):
    row, col, core = (lax.axis_index(a) for a in AX)
    x, y, z = row, col // NZ, col % NZ
    g = jnp.where(core == 0, x, y)
    p = jnp.where(core == 0, y, x)
    place = jnp.stack([g, p, core, row * NY * NZ + col]).astype(jnp.int32)

    shares = small_shares(cycle_map, amp_map, cycle_integrals.T, amplitudes)
    [amplitudes] = after([amplitudes], shares[0])
    shares = [shares[0]] + [shift_g(shares[4 - d], -d) for d in (1, 2, 3)]
    mine, *sends = amp_shares(place, amp_map, amplitudes)
    both = group_order(place, after(shares, mine))

    f, b = shift_z(both, 1), shift_z(both, -1)
    sends = after(sends, both)
    blocks = [mine] + [shift_g(sends[d - 1], d) for d in (1, 2, 3)]
    f2, b2 = shift_z(f, 1), shift_z(b, -1)
    pieces = [both, b, f, b2, f2]
    early = part_early(after(pieces, *blocks[1:]))
    f3, b3 = shift_z(f2, 1), shift_z(b2, -1)
    ef, eb = shift_p(early, 1), shift_p(early, -1)
    half = both.shape[0] // 2
    pieces += [b3, f3, shift_z(b3[:half], -1), shift_z(f3[half:], 1)]
    late, win = part_late(pieces)
    lf, lb = shift_p(late, 1), shift_p(late, -1)
    half = EARLY // 2
    early = [early, eb, shift_p(eb[:half], -1), shift_p(ef[half:], 1), ef]
    half = LATE // 2
    late = [late, lb, shift_p(lb[:half], -1), shift_p(lf[half:], 1), lf]

    here = lax.broadcasted_iota(jnp.int32, (QW, 1), 0)
    rest = here - 4 * EARLY
    soon = rest < 0
    turn = jnp.where(soon, here // EARLY, rest // LATE)
    spot = jnp.where(soon, here % EARLY // 32, EARLY // 32 + rest % LATE // 32)
    hg, hw = here // 8 % 4, here % 8
    turn_here = (hg - p) % 4
    at = jnp.where(soon, turn_here * EARLY, 4 * EARLY + turn_here * LATE - EARLY) + spot * 32
    there = lax.broadcasted_iota(jnp.int32, (1, QW), 1)
    order = (at + (g + turn) % 4 * 8 + hw == there).astype(BF)
    hp = (p + turn) % 4
    hx, hy = jnp.where(core == 0, hg, hp), jnp.where(core == 0, hp, hg)
    hz = (z + jnp.where(spot % 2 == 1, (spot + 1) // 2, 8 - spot // 2)) % NZ
    there = lax.broadcasted_iota(jnp.int32, (1, QW // 2), 1) + core * (QW // 2)
    final = (hx * 256 + hy * 64 + hz * 8 + hw == there).astype(BF)

    away, own = dressed_first(blocks, early)
    [win] = after([win], late[2])
    wf, wb = shift_p(win, 1), shift_p(win, -1)
    *away, total = dressed_last(blocks, late, away, own)
    back = [shift_g(away[d - 1], -d) for d in (1, 2, 3)]
    for value in back:
        total = total + value.astype(F32)
    inner = inner_call(total, swap_core(total), order)
    inners = [shift_g(inner, d) for d in (1, 2, 3)]
    half = win.shape[0] // 2
    rights = [win, wb, shift_p(wb[:half], -1), shift_p(wf[half:], 1), wf]
    dressed = jnp.dot(inner, final, preferred_element_type=F32).astype(BF)

    outs = {}
    for d in (2, 1, 3):
        [value] = quadratic_blocks([inners[d - 1]], rights)
        outs[d] = shift_g(value, -d)
    [outs[0]] = quadratic_blocks([inner], rights)
    quadratic = place_blocks(place, {0: outs[0]})
    quadratic = place_blocks(place, {2: outs[2]}, quadratic)
    quadratic = place_blocks(place, {1: outs[1], 3: outs[3]}, quadratic)
    return (dressed, quadratic)


def solution(mesh):
    placed = (P(("row", "col"), "rep"), P("rep", ("row", "col")), P(("row", "col"), "rep"), P())
    return jax.shard_map(
        body,
        mesh=mesh,
        in_specs=placed,
        out_specs=(P(("row", "col"), "rep"), P(("row", "col"), "rep")),
        check_vma=False,
    )
```

```python
import functools

import jax
import jax.numpy as jnp
from jax import lax
from jax.experimental import pallas as pl
from jax.experimental.pallas import tpu as pltpu
from jax.sharding import PartitionSpec as P

TB = 128
WD = 8
NX, NY, NZ = 4, 4, 8
AX = ("row", "col", "rep")
F32, BF = jnp.float32, jnp.bfloat16
ROWS = 128
HALF = 8192
PART = HALF // 4
QW = 1024
EARLY = 5 * 32
LATE = 3 * 32
VMEM = pl.BlockSpec(memory_space=pltpu.VMEM)
PARAMS = pltpu.CompilerParams(vmem_limit_bytes=8 * 2**20)
WIDE = pltpu.CompilerParams(vmem_limit_bytes=16 * 2**20)


def ident(x, y, z, c):
    return ((x % NX) * NY * NZ + (y % NY) * NZ + z % NZ) * 2 + c


def every():
    return [(x, y, z, c) for x in range(NX) for y in range(NY) for z in range(NZ) for c in (0, 1)]


def shift_z(value, step):
    return lax.ppermute(value, AX, [(ident(x, y, z, c), ident(x, y, z + step, c)) for x, y, z, c in every()])


def shift_plane(value, step, swapped):
    pairs = []
    for x, y, z, c in every():
        if (c == 0) != swapped:
            pairs.append((ident(x, y, z, c), ident(x + step, y, z, c)))
        else:
            pairs.append((ident(x, y, z, c), ident(x, y + step, z, c)))
    return lax.ppermute(value, AX, pairs)


def shift_g(value, step):
    return shift_plane(value, step, False)


def shift_p(value, step):
    return shift_plane(value, step, True)


def swap_core(value):
    return lax.ppermute(value, AX, [(ident(x, y, z, c), ident(x, y, z, 1 - c)) for x, y, z, c in every()])


def cost(flops, moved):
    return pl.CostEstimate(flops=flops, bytes_accessed=moved, transcendentals=0)


def shares_kernel(cyc_map_in, amp_map_in, cyc_in, amp, *refs):
    outs, rows, both, half_map, amp_map, cyc, sem = refs[:4], *refs[4:]
    row, col, core = (lax.axis_index(a) for a in AX)
    g = jnp.where(core == 0, row, col // NZ)
    tiles = HALF // TB
    mine = cyc_map_in.at[pl.ds(pl.multiple_of(core * tiles, tiles), tiles), :]
    pairs = [(mine, half_map), (amp_map_in, amp_map), (cyc_in, cyc), (amp.at[0:16, :], rows)]
    copies = [pltpu.make_async_copy(pairs[i][0], pairs[i][1], sem.at[i]) for i in range(4)]
    for copy in copies:
        copy.start()
    for copy in copies:
        copy.wait()
    half_map = half_map[...].astype(F32)
    lane = lax.broadcasted_iota(jnp.int32, half_map.shape, 1)
    keep = jnp.sum(jnp.where(lane == row * NY * NZ + col, half_map, 0.0), axis=1, keepdims=True)
    keep_window = amp_map[...].astype(F32)
    for t in range(tiles):
        at = slice(t * TB, (t + 1) * TB)
        top = cyc[:, at].astype(F32) * keep[t : t + 1, :]
        low = rows[:WD, at].astype(F32) * keep_window[:, t : t + 1]
        both[:, at] = jnp.concatenate([top, low], 0).astype(BF)
    for d in range(4):
        share = pl.multiple_of(lax.rem(g + d, 4) * PART, PART)
        outs[d][...] = both[:, pl.ds(share, PART)]


def small_shares(cycle_map, amp_map, cyc, amplitudes):
    return pl.pallas_call(
        shares_kernel,
        out_shape=[jax.ShapeDtypeStruct((2 * WD, PART), BF)] * 4,
        in_specs=[pl.BlockSpec(memory_space=pl.ANY)] * 4,
        out_specs=[VMEM] * 4,
        scratch_shapes=[
            pltpu.VMEM((16, HALF), BF),
            pltpu.VMEM((16, HALF), BF),
            pltpu.VMEM((HALF // TB, 128), jnp.int32),
            pltpu.VMEM((1, HALF // TB), jnp.int32),
            pltpu.VMEM((WD, HALF), BF),
            pltpu.SemaphoreType.DMA((4,)),
        ],
        compiler_params=pltpu.CompilerParams(vmem_limit_bytes=60 * 2**20),
        cost_estimate=cost(0, 600_000),
    )(cycle_map, amp_map, cyc, amplitudes)


def group_kernel(place, *refs):
    pieces, out = refs[:4], refs[4]
    rows = 8 * WD
    here = lax.broadcasted_iota(jnp.int32, (rows, rows), 1)
    there = lax.broadcasted_iota(jnp.int32, (rows, rows), 0)
    member = (here // 16 + place[0]) % 4
    at = member // 2 * 32 + here // 8 % 2 * 16 + member % 2 * 8 + here % 8
    order = (at == there).astype(F32).astype(BF)
    value = jnp.concatenate([ref[...] for ref in pieces], 0)
    out[...] = jnp.dot(order, value, preferred_element_type=F32).astype(BF)


def group_order(place, pieces):
    return pl.pallas_call(
        group_kernel,
        out_shape=jax.ShapeDtypeStruct((8 * WD, PART), BF),
        grid_spec=pltpu.PrefetchScalarGridSpec(
            num_scalar_prefetch=1, grid=(), in_specs=[VMEM] * 4, out_specs=VMEM
        ),
        compiler_params=PARAMS,
        cost_estimate=cost(2 * 64 * 64 * PART, 600_000),
    )(place, *pieces)


def late_kernel(*refs):
    outs = refs[9:]
    at = 0
    for ref in refs[:9]:
        for rows in range(0, ref.shape[0], 32):
            if at >= EARLY:
                outs[0][at - EARLY : at - EARLY + 16, :] = ref[rows : rows + 16, :]
            outs[1][at : at + 16, :] = ref[rows + 16 : rows + 32, :]
            at += 16


def early_kernel(*refs):
    at = 0
    for ref in refs[:5]:
        for rows in range(0, ref.shape[0], 32):
            refs[5][at : at + 16, :] = ref[rows : rows + 16, :]
            at += 16


def part_early(pieces):
    return pl.pallas_call(
        early_kernel,
        out_shape=jax.ShapeDtypeStruct((EARLY, PART), BF),
        in_specs=[VMEM] * 5,
        out_specs=VMEM,
        compiler_params=PARAMS,
        cost_estimate=cost(0, 1_300_000),
    )(*pieces)


def part_late(pieces):
    return pl.pallas_call(
        late_kernel,
        out_shape=[
            jax.ShapeDtypeStruct((LATE, PART), BF),
            jax.ShapeDtypeStruct((EARLY + LATE, PART), BF),
        ],
        in_specs=[VMEM] * 9,
        out_specs=[VMEM] * 2,
        compiler_params=PARAMS,
        cost_estimate=cost(0, 4_000_000),
    )(*pieces)


def amp_kernel(place, amp_map, *refs):
    ins, outs = refs[:4], refs[4:]
    for d in range(4):
        share = lax.rem(place[0] + d, 4)
        for t in range(PART // TB):
            keep = amp_map[0, share * 16 + t].astype(BF)
            outs[d][:, t * TB : (t + 1) * TB] = ins[d][:, t * TB : (t + 1) * TB] * keep


def amp_shares(place, amp_map, amplitudes):
    block = 32

    def source(d):
        return pl.BlockSpec((block, PART), lambda i, place, amp_map: (i, lax.rem(place[0] + d, 4)))

    return pl.pallas_call(
        amp_kernel,
        out_shape=[jax.ShapeDtypeStruct((ROWS, PART), BF)] * 4,
        grid_spec=pltpu.PrefetchScalarGridSpec(
            num_scalar_prefetch=2,
            grid=(ROWS // block,),
            in_specs=[source(d) for d in range(4)],
            out_specs=[pl.BlockSpec((block, PART), lambda i, place, amp_map: (i, 0))] * 4,
        ),
        compiler_params=PARAMS,
        cost_estimate=cost(0, 4_000_000),
    )(place, amp_map, *[amplitudes] * 4)


def product(blocks, cyc):
    left = jnp.concatenate([blocks[d][...] for d in (1, 2, 3, 0)], 0)
    right = jnp.concatenate([ref[...] for ref in cyc], 0)
    return lax.dot_general(left, right, (((1,), (1,)), ((), ())), preferred_element_type=F32)


def dressed_first_kernel(*refs):
    value = product(refs[:4], refs[4:9])
    refs[9][...] = value[: 3 * ROWS].astype(BF)
    refs[10][...] = value[3 * ROWS :]


def dressed_first(blocks, cyc):
    return pl.pallas_call(
        dressed_first_kernel,
        out_shape=[
            jax.ShapeDtypeStruct((3 * ROWS, 4 * EARLY), BF),
            jax.ShapeDtypeStruct((ROWS, 4 * EARLY), F32),
        ],
        in_specs=[VMEM] * 9,
        out_specs=[VMEM] * 2,
        compiler_params=WIDE,
        cost_estimate=cost(2 * 512 * PART * 4 * EARLY, 6_000_000),
    )(*blocks, *cyc)


def dressed_last_kernel(*refs):
    away, early, outs, own = refs[9], refs[10], refs[11:14], refs[14]
    edge = 4 * EARLY
    value = product(refs[:4], refs[4:9])
    for d in range(3):
        rows = slice(d * ROWS, (d + 1) * ROWS)
        outs[d][:, :edge] = away[rows, :]
        outs[d][:, edge:] = value[rows].astype(BF)
    own[:, :edge] = early[...]
    own[:, edge:] = value[3 * ROWS :]


def dressed_last(blocks, cyc, away, early):
    return pl.pallas_call(
        dressed_last_kernel,
        out_shape=[jax.ShapeDtypeStruct((ROWS, QW), BF)] * 3 + [jax.ShapeDtypeStruct((ROWS, QW), F32)],
        in_specs=[VMEM] * 11,
        out_specs=[VMEM] * 4,
        compiler_params=WIDE,
        cost_estimate=cost(2 * 512 * PART * 4 * LATE, 6_000_000),
    )(*blocks, *cyc, away, early)


def inner_kernel(mine, other, order, out):
    value = other[...]
    high = value.astype(BF)
    rest = value - high.astype(F32)
    middle = rest.astype(BF)
    low = (rest - middle.astype(F32)).astype(BF)
    moved = jnp.dot(jnp.concatenate([high, middle, low], 0), order[...], preferred_element_type=F32)
    moved = moved[:ROWS] + moved[ROWS : 2 * ROWS] + moved[2 * ROWS :]
    out[...] = (mine[...] + moved).astype(BF)


def inner_call(mine, other, order):
    return pl.pallas_call(
        inner_kernel,
        out_shape=jax.ShapeDtypeStruct((ROWS, QW), BF),
        in_specs=[VMEM] * 3,
        out_specs=VMEM,
        compiler_params=PARAMS,
        cost_estimate=cost(6 * ROWS * QW * QW, 4_000_000),
    )(mine, other, order)


def quadratic_kernel(count, *refs):
    lefts, rights, out, held, sem = refs[:count], refs[count : count + 5], *refs[count + 5 :]
    left = jnp.concatenate([ref[...] for ref in lefts], 0)
    mine, above, half, other, below = rights
    middle = half.shape[0]
    wide = 512
    copies = []
    for n in range(0, PART, wide):
        cols = slice(n, n + wide)
        right = [mine[:EARLY, cols], above[:EARLY, cols], half[:, cols], other[: EARLY - middle, cols]]
        right += [below[:EARLY, cols], mine[EARLY:, cols], above[EARLY:, cols]]
        right += [other[EARLY - middle :, cols], below[EARLY:, cols]]
        value = jnp.dot(left, jnp.concatenate(right, 0), preferred_element_type=F32).astype(BF)
        held[:, cols] = value
        copies.append(pltpu.make_async_copy(held.at[:, cols], out.at[:, cols], sem.at[n // wide]))
        copies[-1].start()
    for copy in copies:
        copy.wait()


def quadratic_blocks(lefts, rights):
    count = len(lefts)
    return pl.pallas_call(
        functools.partial(quadratic_kernel, count),
        out_shape=[jax.ShapeDtypeStruct((ROWS, PART), BF)] * count,
        in_specs=[VMEM] * (count + 5),
        out_specs=[pl.BlockSpec(memory_space=pl.ANY)] * count,
        scratch_shapes=[pltpu.VMEM((ROWS, PART), BF), pltpu.SemaphoreType.DMA((4,))],
        compiler_params=WIDE,
        cost_estimate=cost(2 * count * ROWS * QW * PART, 5_000_000),
    )(*lefts, *rights)


def place_kernel(ds, place, *refs):
    ins, out, held, sem = refs[: len(ds)], refs[-3], refs[-2], refs[-1]
    chunks = [(k, slice(i * 32, i * 32 + 32)) for k in range(len(ds)) for i in range(4)]
    copies = []
    for n, (k, rows) in enumerate(chunks):
        copies.append(pltpu.make_async_copy(ins[k].at[rows, :], held.at[k, rows, :], sem.at[n]))
    for copy in copies:
        copy.start()
    later = []
    for n, (k, rows) in enumerate(chunks):
        at = pl.multiple_of(lax.rem(place[0] + ds[k], 4) * PART, PART)
        copies[n].wait()
        to = out.at[rows, pl.ds(at, PART)]
        later.append(pltpu.make_async_copy(held.at[k, rows, :], to, sem.at[len(chunks) + n]))
        later[-1].start()
    for copy in later:
        copy.wait()


def place_blocks(place, blocks, out=None):
    anywhere = pl.BlockSpec(memory_space=pl.ANY)
    ds = tuple(blocks)
    operands = [place] + [blocks[d] for d in ds] + ([] if out is None else [out])
    return pl.pallas_call(
        functools.partial(place_kernel, ds),
        out_shape=jax.ShapeDtypeStruct((ROWS, HALF), BF),
        grid_spec=pltpu.PrefetchScalarGridSpec(
            num_scalar_prefetch=1,
            grid=(),
            in_specs=[anywhere] * (len(operands) - 1),
            out_specs=anywhere,
            scratch_shapes=[
                pltpu.VMEM((len(ds), ROWS, PART), BF),
                pltpu.SemaphoreType.DMA((8 * len(ds),)),
            ],
        ),
        input_output_aliases={} if out is None else {len(operands) - 1: 0},
        compiler_params=PARAMS,
        cost_estimate=cost(0, 1_000_000 * len(ds)),
    )(*operands)


def after(values, *others):
    count = len(values)
    return lax.optimization_barrier(tuple(values) + others)[:count]


def body(amplitudes, cycle_integrals, amp_map, cycle_map):
    row, col, core = (lax.axis_index(a) for a in AX)
    x, y, z = row, col // NZ, col % NZ
    g = jnp.where(core == 0, x, y)
    p = jnp.where(core == 0, y, x)
    place = jnp.stack([g, p, core, row * NY * NZ + col]).astype(jnp.int32)

    shares = small_shares(cycle_map, amp_map, cycle_integrals.T, amplitudes)
    [amplitudes] = after([amplitudes], shares[0])
    shares = [shares[0]] + [shift_g(shares[4 - d], -d) for d in (1, 2, 3)]
    mine, *sends = amp_shares(place, amp_map, amplitudes)
    both = group_order(place, after(shares, mine))

    f, b = shift_z(both, 1), shift_z(both, -1)
    sends = after(sends, both)
    blocks = [mine] + [shift_g(sends[d - 1], d) for d in (1, 2, 3)]
    f2, b2 = shift_z(f, 1), shift_z(b, -1)
    pieces = [both, b, f, b2, f2]
    early = part_early(after(pieces, *blocks[1:]))
    f3, b3 = shift_z(f2, 1), shift_z(b2, -1)
    ef, eb = shift_p(early, 1), shift_p(early, -1)
    half = both.shape[0] // 2
    pieces += [b3, f3, shift_z(b3[:half], -1), shift_z(f3[half:], 1)]
    late, win = part_late(pieces)
    lf, lb = shift_p(late, 1), shift_p(late, -1)
    half = EARLY // 2
    early = [early, eb, shift_p(eb[:half], -1), shift_p(ef[half:], 1), ef]
    half = LATE // 2
    late = [late, lb, shift_p(lb[:half], -1), shift_p(lf[half:], 1), lf]

    here = lax.broadcasted_iota(jnp.int32, (QW, 1), 0)
    rest = here - 4 * EARLY
    soon = rest < 0
    turn = jnp.where(soon, here // EARLY, rest // LATE)
    spot = jnp.where(soon, here % EARLY // 32, EARLY // 32 + rest % LATE // 32)
    hg, hw = here // 8 % 4, here % 8
    turn_here = (hg - p) % 4
    at = jnp.where(soon, turn_here * EARLY, 4 * EARLY + turn_here * LATE - EARLY) + spot * 32
    there = lax.broadcasted_iota(jnp.int32, (1, QW), 1)
    order = (at + (g + turn) % 4 * 8 + hw == there).astype(BF)
    hp = (p + turn) % 4
    hx, hy = jnp.where(core == 0, hg, hp), jnp.where(core == 0, hp, hg)
    hz = (z + jnp.where(spot % 2 == 1, (spot + 1) // 2, 8 - spot // 2)) % NZ
    there = lax.broadcasted_iota(jnp.int32, (1, QW // 2), 1) + core * (QW // 2)
    final = (hx * 256 + hy * 64 + hz * 8 + hw == there).astype(BF)

    away, own = dressed_first(blocks, early)
    [win] = after([win], late[2])
    wf, wb = shift_p(win, 1), shift_p(win, -1)
    *away, total = dressed_last(blocks, late, away, own)
    back = [shift_g(away[d - 1], -d) for d in (1, 2, 3)]
    for value in back:
        total = total + value.astype(F32)
    inner = inner_call(total, swap_core(total), order)
    inners = [shift_g(inner, d) for d in (1, 2, 3)]
    half = win.shape[0] // 2
    rights = [win, wb, shift_p(wb[:half], -1), shift_p(wf[half:], 1), wf]
    dressed = jnp.dot(inner, final, preferred_element_type=F32).astype(BF)

    outs = {}
    for d in (2, 1, 3):
        [value] = quadratic_blocks([inners[d - 1]], rights)
        outs[d] = shift_g(value, -d)
    [outs[0]] = quadratic_blocks([inner], rights)
    quadratic = place_blocks(place, {0: outs[0]})
    quadratic = place_blocks(place, {2: outs[2]}, quadratic)
    quadratic = place_blocks(place, {1: outs[1], 3: outs[3]}, quadratic)
    return (dressed, quadratic)


def solution(mesh):
    placed = (P(("row", "col"), "rep"), P("rep", ("row", "col")), P(("row", "col"), "rep"), P())
    return jax.shard_map(
        body,
        mesh=mesh,
        in_specs=placed,
        out_specs=(P(("row", "col"), "rep"), P(("row", "col"), "rep")),
        check_vma=False,
    )
```
